1024 devices in a mesh: pipe: 16 (over y, core), expert: 16 (over x_lo, z), dp: 4 (over x_hi).
Axes of the slice: x: 8 (x_hi: 4, x_lo: 2; x = x_hi * 2 + x_lo), y: 8, z: 8, core: 2. Of those that a mesh axis runs over, the one named last changes fastest.
Arguments:
- tokens: bfloat16 [16, 2048, 4096], P('pipe', 'expert'), may hold values from -6 to 6
- modality: int32 [16, 2048], P('pipe', 'expert'), may hold values 0 or 1
- routes: int32 [16, 2048, 1], P('pipe', 'expert'), may hold values from 0 to 3; in each aligned block of 128 rows (0 to 127, 128 to 255, ..., all dimensions but the last counted through in order) at most 64 rows name the same one
- norm_gain: float32 [4096], replicated, may hold values from 0.5 to 1.5
- router: bfloat16 [2, 4096, 4], replicated, may hold values from -0.09375 to 0.09375
- gate_weight: bfloat16 [16, 4096, 7168], P('pipe', 'dp', 'expert'), may hold values from -0.09375 to 0.09375
- down_weight: bfloat16 [16, 7168, 4096], P('pipe', 'expert', 'dp'), may hold values from -0.125 to 0.125
Outputs:
- section_output: bfloat16 [16, 2048, 4096], P('pipe', 'expert', 'dp')
The draws below stay inside these ranges and needn't reach their ends.
Inputs may be any that keep to these rules, and one draw needn't show every extreme that they name: `routes`: among the rows of one device (aligned blocks of 128 rows of a section) no expert is named more than 64 times, and in every draw some device names one expert exactly 64 times.
All inputs are finite; a program needn't handle non-finite values. No bound on the sum of `modality` on one device may be relied on, other than what follows from the above.
Results may differ from the reference program's by a relative error of at most 0.0036.
Values may be sent and summed in bfloat16 or wider, within the bound.
A program may use at most 32 MiB of HBM per device.

```python
import math
import jax
import jax.numpy as jnp
import numpy as np
from jax import lax

D = 4096
H = 1792
EXPERTS = 4
MODALITIES = 2
TOK_DEV = 128
CAP = 64
TOKENS = 2048
N_PIPE = 16
N_EXPERT = 16


def set_ends(result, stream_key, least, top_value):
    longest = result.shape.index(max(result.shape))
    spots = []
    for shift in (0, 1):
        where = [jax.random.randint(jax.random.fold_in(stream_key, axis), (), 0, length) for axis, length in enumerate(result.shape)]
        where[longest] = (where[longest] + shift) % result.shape[longest]
        spots.append(tuple(where))
    return result.at[spots[0]].set(least).at[spots[1]].set(top_value)


def shard_levels(key, dims, pieces, smallest, largest):
    def one(dim, blocks):
        draws = jax.random.uniform(jax.random.fold_in(jax.random.fold_in(key, 6), dim), (blocks,), jnp.float32, smallest / len(pieces), largest / len(pieces))
        return jnp.repeat(jnp.exp(draws), dims[dim] // blocks).reshape((-1,) + (1,) * (len(dims) - dim - 1))

    loudness = one(*pieces[0])
    for cut in pieces[1:]:
        loudness = loudness * one(*cut)
    return loudness


def assign_block(own_key, own, number, rows, count, top, reach, lean):
    order = jax.random.permutation(own_key, count)
    packed, common = portions_of(count, rows * top, reach, lean, True), portions_of(count, rows * top, reach, lean, False)
    places = jnp.arange(count)

    def named(lengths, turn):
        used = int((lengths > 0).sum())
        fixed = max(1, used // 4)
        shifted = fixed + (places - fixed + turn * (used - fixed)) % max(1, count - fixed)
        return jnp.zeros((count,), jnp.int32).at[order[jnp.where(places < fixed, places, shifted)]].set(jnp.asarray(lengths, jnp.int32))

    lengths = jnp.where(number % 4 == 0, named(packed, number // 4), named(common, number - number // 4 - 1))
    mixed = jax.random.permutation(jax.random.fold_in(own, 3), count)
    source_of, taker = mixed[0:count // 2 * 2:2], mixed[1:count // 2 * 2:2]
    room = jnp.minimum(lengths[source_of] - 1, reach - lengths[taker]) // 2
    room = jnp.where((source_of == order[0]) | (taker == order[0]) | (lengths[taker] == 0), 0, jnp.maximum(room, 0))
    shifted = jax.random.randint(jax.random.fold_in(own, 4), (count // 2,), 0, 1 << 20) % (room + 1)
    lengths = lengths.at[source_of].add(-shifted).at[taker].add(shifted)
    items = jnp.searchsorted(jnp.cumsum(lengths), jnp.arange(rows * top), side="right").astype(jnp.int32)
    listing = items.reshape(top, rows).T
    listing = listing[jax.random.permutation(jax.random.fold_in(own, 1), rows)]
    turn = jax.random.randint(jax.random.fold_in(own, 2), (rows, 1), 0, top)
    return jnp.take_along_axis(listing, (jnp.arange(top)[None, :] + turn) % top, axis=1)


def portions_of(count, total, most, slope, full):
    portions = [(1 << 20) // math.isqrt(grade ** slope) + 1 for grade in range(1, count + 1)]
    largest = most if full else min(most, max(-(-total // count), total * portions[0] // sum(portions)))
    least = 1 if total - largest >= count - 1 else 0
    given, spare = [largest] + [least] * (count - 1), total - largest - least * (count - 1)
    while spare > 0:
        free = [i for i in range(1, count) if given[i] < largest] or [i for i in range(1, count) if given[i] < most]
        pool, budget = sum([portions[i] for i in free]), spare
        for i in free:
            addition = min(most - given[i], max(1, budget * portions[i] // pool), spare)
            given[i] = given[i] + addition
            spare = spare - addition
    return np.array(given)


def noise(stream_key, shape, width, limit, shards=(), kind=jnp.bfloat16):
    gain = shard_levels(stream_key, shape, shards, -0.22, 0.18) if shards else 1.0
    result = jax.random.normal(stream_key, shape, jnp.float32) * width * gain
    return jnp.minimum(jnp.maximum(result, -limit), limit).astype(kind)


def setup_inputs(seed: int = 0) -> dict:
    key_list = jax.random.split(jax.random.key(seed), 8)
    tokens = noise(key_list[0], (N_PIPE, TOKENS, D), 1.0, 6.0, ((0, 16), (1, 16)))
    modality = set_ends((jax.random.randint(key_list[1], (N_PIPE, TOKENS), 0, 2) < 1).astype(jnp.int32), jax.random.fold_in(key_list[1], 1), 0, 1)
    routes_keys = jax.random.split(jax.random.fold_in(key_list[2], 1), N_PIPE * TOKENS // TOK_DEV)
    routes_turns = jax.random.permutation(jax.random.fold_in(key_list[2], 3), N_PIPE * TOKENS // TOK_DEV)
    routes = jax.vmap(lambda own, number: assign_block(jax.random.fold_in(key_list[2], 2), own, number, TOK_DEV, EXPERTS, 1, CAP, 2))(routes_keys, routes_turns).reshape((N_PIPE, TOKENS, 1))
    norm_gain = jnp.clip(1.0 + 0.1 * jax.random.normal(key_list[3], (D,), jnp.float32), 0.5, 1.5)
    router = noise(key_list[4], (MODALITIES, D, EXPERTS), D ** -0.5, 0.09375)
    gate_weight = noise(key_list[5], (N_PIPE, D, EXPERTS * H), D ** -0.5, 0.09375, ((0, 16), (1, 4), (2, 16)))
    down_weight = noise(key_list[6], (N_PIPE, EXPERTS * H, D), H ** -0.5, 0.125, ((0, 16), (1, 16), (2, 4)))
    return dict(tokens=tokens, modality=modality, routes=routes, norm_gain=norm_gain, router=router, gate_weight=gate_weight, down_weight=down_weight)


epsilon = 1e-06

def reference(tokens, modality, routes, norm_gain, router, gate_weight, down_weight):
    arriving = jnp.roll(tokens, 1, axis=0)
    group_size = N_EXPERT // EXPERTS
    hidden_part = H // group_size

    def one_section(section_args):
        section_rows, token_kind, route_ids, section_gate, section_down = section_args
        stream = section_rows.astype(jnp.float32)
        scale = lax.rsqrt(lax.optimization_barrier(jnp.mean(stream * stream, axis=-1, keepdims=True)) + epsilon)
        normed = (stream * scale * norm_gain).astype(jnp.bfloat16)
        logits = jnp.einsum('td,mde->mte', normed.astype(jnp.float32), router.astype(jnp.float32), precision=lax.Precision.HIGHEST)
        chosen = jnp.where(token_kind[:, None] == 1, logits[1], logits[0])
        route_flat = route_ids[:, 0]
        matches = route_flat[:, None] == jnp.arange(EXPERTS, dtype=jnp.int32)[None, :]
        route_logit = lax.optimization_barrier(jnp.sum(jnp.where(matches, chosen, 0.0), axis=1))
        gate_value = jax.nn.sigmoid(route_logit)
        gate_all = jnp.transpose(section_gate.reshape(D, EXPERTS, H), (1, 0, 2))
        down_all = section_down.reshape(EXPERTS, H, D)

        def one_expert(expert_args):
            expert_id, weight_gate, weight_down = expert_args
            positions = jnp.nonzero(route_flat == expert_id, size=CAP * N_EXPERT, fill_value=TOKENS)[0]
            gathered = jnp.take(normed, positions, axis=0, mode='fill', fill_value=0)
            hidden = jax.nn.silu(jnp.dot(gathered, weight_gate, preferred_element_type=jnp.float32)).astype(jnp.bfloat16)
            group_terms = jnp.einsum('rgh,ghd->grd', hidden.reshape(-1, group_size, hidden_part).astype(jnp.float32), weight_down.reshape(group_size, hidden_part, D).astype(jnp.float32), precision=lax.Precision.HIGHEST)
            rounded = lax.optimization_barrier(group_terms.astype(jnp.bfloat16))
            summed = lax.optimization_barrier(jnp.sum(rounded.astype(jnp.float32), axis=0)).astype(jnp.bfloat16)
            return (summed, positions)
        expert_rows, all_positions = lax.map(one_expert, (jnp.arange(EXPERTS, dtype=jnp.int32), gate_all, down_all))
        combined = jnp.zeros((TOKENS, D), jnp.bfloat16).at[all_positions.reshape(-1)].set(expert_rows.reshape(-1, D), mode='drop')
        return (stream + gate_value[:, None] * combined.astype(jnp.float32)).astype(jnp.bfloat16)
    return lax.map(one_section, (arriving, modality, routes, gate_weight, down_weight))
```

```python
import functools

import jax
import jax.numpy as jnp
from jax import lax
from jax.experimental import pallas as pl
from jax.experimental.pallas import tpu as pltpu
from jax.sharding import PartitionSpec as P

MESH = pl.DeviceIdType.MESH
epsilon = 1e-06
Z = 8
STEPS = 8


def kernel(
    n_pipe, n_dp,
    tokens, modality, routes, gain, router, gate_hbm, down_hbm,
    out,
    tok_v, normed_v, gate_v, down_v, arrived, stat_tx, stat_rx, placer, unplacer, chosen,
    packed, recv, rs_tx, rs_rx, own_sum, hid, term, ret_far, ret_near, fin,
    local_sem, pipe_send, pipe_recv, first_send, forward_send, dispatch_recv,
    sum_send, sum_recv, hid_send, hid_recv, ret_send, far_recv, near_recv, fin_recv,
):
    tok = tok_v.shape[0]
    cap = recv.shape[1] // 2
    part = recv.shape[2]
    piece = rs_rx.shape[2]
    s, j, d = lax.axis_index("pipe"), lax.axis_index("expert"), lax.axis_index("dp")
    xl, z = j // Z, j % Z
    g, p = z // 4, z % 4
    mid = ((p + 1) // 2) % 2
    nd = 2 * (p // 2) - 1
    near, far = (z + nd + Z) % Z, (z - nd + Z) % Z
    across = (z + nd * (1 + mid) + Z) % Z
    second = (z + 2 * nd + Z) % Z
    beside = (z + nd * (1 - 2 * mid) + Z) % Z
    other = 1 - xl
    is_mid = mid == 1
    is_end = mid == 0

    def at(x, zz):
        return (s, x * Z + zz, d)

    def send(src, dst, send_sem, recv_sem, device):
        return pltpu.make_async_remote_copy(
            src_ref=src, dst_ref=dst, send_sem=send_sem, recv_sem=recv_sem,
            device_id=device, device_id_type=MESH,
        )

    def rows(ref, zz, x):
        return ref.at[zz, pl.ds(pl.multiple_of(x * cap, cap), cap)]

    tok_copy = pltpu.make_async_copy(tokens, tok_v, local_sem.at[0])
    gate_copy = pltpu.make_async_copy(gate_hbm, gate_v, local_sem.at[1])
    down_copy = pltpu.make_async_copy(down_hbm, down_v, local_sem.at[2])
    tok_copy.start()

    barrier = pltpu.get_barrier_semaphore()
    partners = [
        ((s + 1) % n_pipe, j, d),
        ((s + n_pipe - 1) % n_pipe, j, d),
        at(other, z), at(xl, near), at(xl, far), at(xl, second), at(other, second), at(other, beside),
    ] + [(s, j, (d + k) % n_dp) for k in range(1, n_dp)]
    for device in partners:
        pl.semaphore_signal(barrier, inc=1, device_id=device, device_id_type=MESH)
    gate_copy.start()
    down_copy.start()

    route_row = routes[...]
    hits = (lax.broadcasted_iota(jnp.int32, (8, tok), 0) == route_row).astype(jnp.float32)
    before = (
        lax.broadcasted_iota(jnp.int32, (tok, tok), 0) < lax.broadcasted_iota(jnp.int32, (tok, tok), 1)
    ).astype(jnp.bfloat16)
    earlier = jnp.dot(hits.astype(jnp.bfloat16), before, preferred_element_type=jnp.float32)
    rank = jnp.sum(hits * earlier, axis=0, keepdims=True)
    slot_row = route_row.astype(jnp.float32) * cap + rank
    slots = lax.broadcasted_iota(jnp.int32, (4 * cap, tok), 0).astype(jnp.float32)
    placer[...] = (slots == slot_row).astype(jnp.bfloat16)
    slot_col = jnp.transpose(jnp.broadcast_to(slot_row, (tok, tok)))[:, 0:1]
    slots = lax.broadcasted_iota(jnp.int32, (tok, 4 * cap), 1).astype(jnp.float32)
    unplacer[...] = (slots == slot_col).astype(jnp.bfloat16)
    pick_row = (modality[...] * 4 + route_row).astype(jnp.float32)
    pick_col = jnp.transpose(jnp.broadcast_to(pick_row, (tok, tok)))[:, 0:1]
    lanes = lax.broadcasted_iota(jnp.int32, (tok, 128), 1).astype(jnp.float32)
    chosen[...] = (lanes == pick_col).astype(jnp.float32)

    pl.semaphore_wait(barrier, len(partners))

    following = ((s + 1) % n_pipe, j, d)
    own_columns = pl.ds(pl.multiple_of(d * part, part), part)
    raw_copy = send(tokens.at[:, own_columns], arrived, pipe_send.at[0], pipe_recv.at[0], following)
    raw_copy.start()

    stat_tx[...] = jnp.zeros_like(stat_tx)
    tok_copy.wait()

    def norm_rows(i, carry):
        block = pl.ds(pl.multiple_of(i * 16, 16), 16)
        x = tok_v[block, :].astype(jnp.float32)
        scale = lax.rsqrt(jnp.mean(x * x, axis=-1, keepdims=True) + epsilon)
        normed_v[block, :] = (x * scale * gain[...]).astype(jnp.bfloat16)
        stat_tx[block, 8:9] = scale
        return carry

    lax.fori_loop(0, tok // 16, norm_rows, 0)
    for kind in range(2):
        stat_tx[:, 4 * kind : 4 * kind + 4] = lax.dot_general(
            normed_v[...], router[kind], (((1,), (1,)), ((), ())), preferred_element_type=jnp.float32
        )
    stat_copy = send(stat_tx, stat_rx, pipe_send.at[1], pipe_recv.at[1], following)
    stat_copy.start()
    raw_copy.wait_recv()
    stat_copy.wait_recv()

    scale = stat_rx[:, 8:9]
    normed = (arrived[...].astype(jnp.float32) * scale * gain[:, own_columns]).astype(jnp.bfloat16)

    def pack(x, group):
        spot = pl.ds(pl.multiple_of((2 * x + group) * cap, cap), cap)
        return jnp.dot(placer[spot, :], normed, preferred_element_type=jnp.float32).astype(jnp.bfloat16)

    packed[0] = pack(other, g)
    cross = send(packed.at[0], rows(recv, z, xl), first_send.at[0], dispatch_recv.at[z, xl], at(other, z))
    cross.start()
    recv[z, pl.ds(pl.multiple_of(xl * cap, cap), cap), :] = pack(xl, g)
    own_far = send(rows(recv, z, xl), rows(recv, z, xl), first_send.at[1], dispatch_recv.at[z, xl], at(xl, far))
    own_near = send(rows(recv, z, xl), rows(recv, z, xl), first_send.at[2], dispatch_recv.at[z, xl], at(xl, near))
    own_far.start()

    @pl.when(is_mid)
    def _():
        own_near.start()

    packed[1] = pack(xl, 1 - g)
    ext_own = send(packed.at[1], rows(recv, z, xl), first_send.at[3], dispatch_recv.at[z, xl], at(xl, across))
    ext_own.start()
    packed[2] = pack(other, 1 - g)
    ext_other = send(packed.at[2], rows(recv, z, xl), first_send.at[4], dispatch_recv.at[z, xl], at(other, across))
    ext_other.start()

    relay_far = send(rows(recv, z, other), rows(recv, z, other), first_send.at[5], dispatch_recv.at[z, other], at(xl, far))
    relay_near = send(rows(recv, z, other), rows(recv, z, other), first_send.at[6], dispatch_recv.at[z, other], at(xl, near))
    relay_far.wait_recv()
    relay_far.start()

    @pl.when(is_mid)
    def _():
        relay_near.start()

    gate_copy.wait()
    down_copy.wait()

    def source(t):
        late = (1 - mid) * (t // 5)
        usual = (t % 2) * ((t + 1) // 2) - (1 - t % 2) * (t // 2)
        offset = usual * (1 - late) + late * (2 - t)
        return (z + nd * offset + 2 * Z) % Z

    def forward(t, zz, x):
        to_near = mid * (1 - (t % 2) * (1 - t // 7))
        target = (z + nd * (2 * to_near - 1) + Z) % Z
        return send(rows(recv, zz, x), rows(recv, zz, x), forward_send.at[t, x], dispatch_recv.at[zz, x], at(xl, target))

    def forwards(t):
        return (t >= 1) & (is_mid | (t == 1) | (t == 3))

    def sum_copy(t, k):
        q = (d + k) % n_dp
        return send(
            rs_tx.at[t, pl.ds(pl.multiple_of(q * piece, piece), piece)], rs_rx.at[t, k - 1],
            sum_send.at[t, k - 1], sum_recv.at[t, k - 1], (s, j, q),
        )

    def hid_copy(t, k):
        own = hid.at[t, pl.ds(pl.multiple_of(d * piece, piece), piece)]
        return send(own, own, hid_send.at[t, k - 1], hid_recv.at[t, k - 1], (s, j, (d + k) % n_dp))

    def leaf_copy(zz, x):
        return send(rows(ret_near, zz, x), rows(ret_near, zz, x), ret_send.at[zz, x], near_recv.at[zz, x], at(xl, far))

    def up_copy(zz, x):
        return send(rows(ret_near, zz, x), rows(ret_far, zz, x), ret_send.at[zz, x], far_recv.at[zz, x], at(xl, far))

    def down_chain(zz, x):
        return send(rows(ret_far, zz, x), rows(ret_far, zz, x), ret_send.at[zz, x], far_recv.at[zz, x], at(xl, near))

    own_expert = 2 * xl + g

    def home_copy(zz, x):
        return send(rows(ret_far, zz, x), fin.at[own_expert], ret_send.at[zz, x], fin_recv.at[own_expert], at(x, zz))

    def each_step(i, carry):
        @pl.when(i <= 7)
        def _():
            zz = source(i)
            for x in (xl, other):
                @pl.when(i >= 1)
                def _():
                    forward(i, zz, x).wait_recv()

                @pl.when(forwards(i))
                def _():
                    forward(i, zz, x).start()

            terms = lax.dot_general(
                recv[zz], gate_v[...], (((1,), (1,)), ((), ())), preferred_element_type=jnp.float32
            )
            own_sum[i % 2] = terms
            rs_tx[i] = terms.astype(jnp.bfloat16)
            for k in range(1, n_dp):
                sum_copy(i, k).start()

        @pl.when((i >= 1) & (i <= 8))
        def _():
            t = i - 1
            for k in range(1, n_dp):
                sum_copy(t, k).wait_recv()
            mine = pl.ds(pl.multiple_of(d * piece, piece), piece)
            total = own_sum[t % 2, mine, :]
            for k in range(1, n_dp):
                total = total + rs_rx[t, k - 1].astype(jnp.float32)
            hid[t, mine, :] = (total / (1.0 + jnp.exp(-total))).astype(jnp.bfloat16)
            for k in range(1, n_dp):
                hid_copy(t, k).start()

        @pl.when((i >= 2) & (i <= 9))
        def _():
            t = i - 2
            zz = source(t)
            for k in range(1, n_dp):
                hid_copy(t, k).wait_recv()
            term[zz] = jnp.dot(hid[t], down_v[...], preferred_element_type=jnp.float32)

            @pl.when(is_end & ((t == 2) | (t >= 4)))
            def _():
                ret_near[zz] = term[zz].astype(jnp.bfloat16)
                for x in range(2):
                    leaf_copy(zz, x).start()

        @pl.when(is_mid & (i >= 7) & (i <= 10))
        def _():
            zz = (z - nd * (i - 6) + Z) % Z
            for x in range(2):
                leaf_copy(zz, x).wait_recv()
                span = slice(x * cap, (x + 1) * cap)
                ret_near[zz, span] = (term[zz, span] + ret_near[zz, span].astype(jnp.float32)).astype(jnp.bfloat16)
                up_copy(zz, x).start()

        @pl.when(is_mid & (i >= 9) & (i <= 11))
        def _():
            zz = (z + nd * (i - 8) + Z) % Z
            for x in range(2):
                down_chain(zz, x).wait_recv()
                span = slice(x * cap, (x + 1) * cap)
                ret_far[zz, span] = (term[zz, span] + ret_far[zz, span].astype(jnp.float32)).astype(jnp.bfloat16)
                down_chain(zz, x).start()

        @pl.when((is_mid & (i == 8)) | (is_end & (i == 10)))
        def _():
            for x in (other, xl):
                span = pl.ds(pl.multiple_of(x * cap, cap), cap)
                up_copy(z, x).wait_recv()
                ret_far[z, span, :] = (term[z, span, :] + ret_far[z, span, :].astype(jnp.float32)).astype(jnp.bfloat16)

                @pl.when(is_mid)
                def _():
                    leaf_copy(z, x).wait_recv()
                    ret_far[z, span, :] = (
                        ret_far[z, span, :].astype(jnp.float32) + ret_near[z, span, :].astype(jnp.float32)
                    ).astype(jnp.bfloat16)

                if x is other:
                    home_copy(z, other).start()
            fin[own_expert] = ret_far[z, pl.ds(pl.multiple_of(xl * cap, cap), cap), :]

        @pl.when(is_end & (i >= 11))
        def _():
            zz = (z + nd * (i - 10) + Z) % Z
            for x in range(2):
                up_copy(zz, x).wait_recv()
                span = slice(x * cap, (x + 1) * cap)
                ret_far[zz, span] = (term[zz, span] + ret_far[zz, span].astype(jnp.float32)).astype(jnp.bfloat16)
                home_copy(zz, x).start()

        return carry

    lax.fori_loop(0, 13, each_step, 0)

    for x, group in ((other, g), (xl, 1 - g), (other, 1 - g)):
        e = 2 * x + group
        send(fin.at[e], fin.at[e], ret_send.at[0, 0], fin_recv.at[e], at(other, z)).wait_recv()

    gate_value = 1.0 / (1.0 + jnp.exp(-jnp.sum(chosen[...] * stat_rx[...], axis=1, keepdims=True)))
    expert_out = jnp.dot(
        unplacer[...], fin[...].reshape(4 * cap, part), preferred_element_type=jnp.float32
    )
    out[...] = (arrived[...].astype(jnp.float32) + gate_value * expert_out).astype(jnp.bfloat16)

    raw_copy.wait_send()
    stat_copy.wait_send()
    for copy in (cross, own_far, ext_own, ext_other, relay_far):
        copy.wait_send()

    @pl.when(is_mid)
    def _():
        own_near.wait_send()
        relay_near.wait_send()

    def sent(t, carry):
        zz = source(t)

        @pl.when(forwards(t))
        def _():
            for x in range(2):
                forward(t, zz, x).wait_send()

        for k in range(1, n_dp):
            sum_copy(t, k).wait_send()
            hid_copy(t, k).wait_send()

        @pl.when(t >= 1)
        def _():
            for x in range(2):
                leaf_copy(zz, x).wait_send()

        return carry

    lax.fori_loop(0, STEPS, sent, 0)
    home_copy(z, other).wait_send()


def local(tokens, modality, routes, norm_gain, router, gate_weight, down_weight):
    tok, width = tokens.shape[1:]
    n_pipe, n_dp = lax.axis_size("pipe"), lax.axis_size("dp")
    part = width // n_dp
    cap = 2 * tok // router.shape[2]
    hidden = gate_weight.shape[2]
    piece = 2 * cap // n_dp
    bf16, f32 = jnp.bfloat16, jnp.float32
    vmem = pl.BlockSpec(memory_space=pltpu.VMEM)
    anywhere = pl.BlockSpec(memory_space=pl.ANY)
    dma = pltpu.SemaphoreType.DMA
    result = pl.pallas_call(
        functools.partial(kernel, n_pipe, n_dp),
        out_shape=jax.ShapeDtypeStruct((tok, part), bf16),
        in_specs=[anywhere, vmem, vmem, vmem, vmem, anywhere, anywhere],
        out_specs=vmem,
        scratch_shapes=[
            pltpu.VMEM((tok, width), bf16),
            pltpu.VMEM((tok, width), bf16),
            pltpu.VMEM((hidden, part), bf16),
            pltpu.VMEM((hidden, part), bf16),
            pltpu.VMEM((tok, part), bf16),
            pltpu.VMEM((tok, 128), f32),
            pltpu.VMEM((tok, 128), f32),
            pltpu.VMEM((4 * cap, tok), bf16),
            pltpu.VMEM((tok, 4 * cap), bf16),
            pltpu.VMEM((tok, 128), f32),
            pltpu.VMEM((3, cap, part), bf16),
            pltpu.VMEM((STEPS, 2 * cap, part), bf16),
            pltpu.VMEM((STEPS, 2 * cap, hidden), bf16),
            pltpu.VMEM((STEPS, n_dp - 1, piece, hidden), bf16),
            pltpu.VMEM((2, 2 * cap, hidden), f32),
            pltpu.VMEM((STEPS, 2 * cap, hidden), bf16),
            pltpu.VMEM((STEPS, 2 * cap, part), f32),
            pltpu.VMEM((STEPS, 2 * cap, part), bf16),
            pltpu.VMEM((STEPS, 2 * cap, part), bf16),
            pltpu.VMEM((4, cap, part), bf16),
            dma((3,)),
            dma((2,)),
            dma((2,)),
            dma((7,)),
            dma((STEPS, 2)),
            dma((STEPS, 2)),
            dma((STEPS, n_dp - 1)),
            dma((STEPS, n_dp - 1)),
            dma((STEPS, n_dp - 1)),
            dma((STEPS, n_dp - 1)),
            dma((STEPS, 2)),
            dma((STEPS, 2)),
            dma((STEPS, 2)),
            dma((4,)),
        ],
        compiler_params=pltpu.CompilerParams(
            collective_id=0, has_side_effects=True, vmem_limit_bytes=48 * 1024 * 1024
        ),
    )(
        tokens[0],
        modality,
        routes.reshape(1, tok),
        norm_gain.reshape(1, width),
        jnp.transpose(router, (0, 2, 1)),
        jnp.transpose(gate_weight[0]),
        down_weight[0],
    )
    return result[None]


def solution(mesh):
    placed = (
        P("pipe", "expert", None),
        P("pipe", "expert"),
        P("pipe", "expert", None),
        P(),
        P(),
        P("pipe", "dp", "expert"),
        P("pipe", "expert", "dp"),
    )
    return jax.shard_map(
        local, mesh=mesh, in_specs=placed, out_specs=P("pipe", "expert", "dp"), check_vma=False
    )
```

```python
import functools

import jax
import jax.numpy as jnp
from jax import lax
from jax.experimental import pallas as pl
from jax.experimental.pallas import tpu as pltpu
from jax.sharding import PartitionSpec as P

MESH = pl.DeviceIdType.MESH
epsilon = 1e-06
Z = 8
STEPS = 8


def kernel(
    n_pipe, n_dp,
    tokens, modality_hbm, routes_hbm, gain_hbm, router_hbm, gate_hbm, down_hbm,
    out,
    modality, routes, gain, router, tok_v, normed_v, gate_v, down_v, arrived, stat_tx, stat_rx, placer, unplacer, chosen,
    packed, recv, sum_tx, sum_half, sum_rx, own_sum, hid, term, ret_far, ret_near, fin,
    local_sem, pipe_send, pipe_recv, first_send, forward_send, dispatch_recv,
    half_send, half_recv, sum_send, sum_recv, hid_send, hid_recv, relay_send, relay_recv, ret_send, far_recv, near_recv, fin_recv,
):
    tok = tok_v.shape[0]
    cap = recv.shape[1] // 2
    part = recv.shape[2]
    piece = sum_rx.shape[2]
    half = piece // 2
    s, j, d = lax.axis_index("pipe"), lax.axis_index("expert"), lax.axis_index("dp")
    xl, z = j // Z, j % Z
    g, p = z // 4, z % 4
    mid = ((p + 1) // 2) % 2
    nd = 2 * (p // 2) - 1
    near, far = (z + nd + Z) % Z, (z - nd + Z) % Z
    across = (z + nd * (1 + mid) + Z) % Z
    second = (z + 2 * nd + Z) % Z
    beside = (z + nd * (1 - 2 * mid) + Z) % Z
    other = 1 - xl
    is_mid = mid == 1
    is_end = mid == 0

    def at(x, zz):
        return (s, x * Z + zz, d)

    def send(src, dst, send_sem, recv_sem, device):
        return pltpu.make_async_remote_copy(
            src_ref=src, dst_ref=dst, send_sem=send_sem, recv_sem=recv_sem,
            device_id=device, device_id_type=MESH,
        )

    def rows(ref, zz, x):
        return ref.at[zz, pl.ds(pl.multiple_of(x * cap, cap), cap)]

    tok_copy = pltpu.make_async_copy(tokens, tok_v, local_sem.at[0])
    gate_copy = pltpu.make_async_copy(gate_hbm, gate_v, local_sem.at[1])
    down_copy = pltpu.make_async_copy(down_hbm, down_v, local_sem.at[2])
    small = [
        pltpu.make_async_copy(a, b, local_sem.at[3 + k])
        for k, (a, b) in enumerate(((modality_hbm, modality), (routes_hbm, routes), (gain_hbm, gain), (router_hbm, router)))
    ]
    for copy in small:
        copy.start()
    tok_copy.start()

    barrier = pltpu.get_barrier_semaphore()
    partners = [
        ((s + 1) % n_pipe, j, d),
        ((s + n_pipe - 1) % n_pipe, j, d),
        at(other, z), at(xl, near), at(xl, far), at(xl, second), at(other, second), at(other, beside),
    ] + [(s, j, (d + k) % n_dp) for k in (1, n_dp - 1)]
    for device in partners:
        pl.semaphore_signal(barrier, inc=1, device_id=device, device_id_type=MESH)
    gate_copy.start()
    down_copy.start()
    for copy in small:
        copy.wait()

    route_row = routes[...]
    hits = (lax.broadcasted_iota(jnp.int32, (8, tok), 0) == route_row).astype(jnp.float32)
    before = (
        lax.broadcasted_iota(jnp.int32, (tok, tok), 0) < lax.broadcasted_iota(jnp.int32, (tok, tok), 1)
    ).astype(jnp.bfloat16)
    earlier = jnp.dot(hits.astype(jnp.bfloat16), before, preferred_element_type=jnp.float32)
    rank = jnp.sum(hits * earlier, axis=0, keepdims=True)
    slot_row = route_row.astype(jnp.float32) * cap + rank
    slots = lax.broadcasted_iota(jnp.int32, (4 * cap, tok), 0).astype(jnp.float32)
    placer[...] = (slots == slot_row).astype(jnp.bfloat16)
    slot_col = jnp.transpose(jnp.broadcast_to(slot_row, (tok, tok)))[:, 0:1]
    slots = lax.broadcasted_iota(jnp.int32, (tok, 4 * cap), 1).astype(jnp.float32)
    unplacer[...] = (slots == slot_col).astype(jnp.bfloat16)
    pick_row = (modality[...] * 4 + route_row).astype(jnp.float32)
    pick_col = jnp.transpose(jnp.broadcast_to(pick_row, (tok, tok)))[:, 0:1]
    lanes = lax.broadcasted_iota(jnp.int32, (tok, 128), 1).astype(jnp.float32)
    chosen[...] = (lanes == pick_col).astype(jnp.float32)

    pl.semaphore_wait(barrier, len(partners))

    following = ((s + 1) % n_pipe, j, d)
    own_columns = pl.ds(pl.multiple_of(d * part, part), part)
    raw_copy = send(tokens.at[:, own_columns], arrived, pipe_send.at[0], pipe_recv.at[0], following)
    raw_copy.start()

    stat_tx[...] = jnp.zeros_like(stat_tx)
    tok_copy.wait()

    def norm_rows(i, carry):
        block = pl.ds(pl.multiple_of(i * 16, 16), 16)
        x = tok_v[block, :].astype(jnp.float32)
        scale = lax.rsqrt(jnp.mean(x * x, axis=-1, keepdims=True) + epsilon)
        normed_v[block, :] = (x * scale * gain[...]).astype(jnp.bfloat16)
        stat_tx[block, 8:9] = scale
        return carry

    lax.fori_loop(0, tok // 16, norm_rows, 0)
    for kind in range(2):
        stat_tx[:, 4 * kind : 4 * kind + 4] = lax.dot_general(
            normed_v[...], router[kind], (((1,), (1,)), ((), ())), preferred_element_type=jnp.float32
        )
    stat_copy = send(stat_tx, stat_rx, pipe_send.at[1], pipe_recv.at[1], following)
    stat_copy.start()
    raw_copy.wait_recv()
    stat_copy.wait_recv()

    scale = stat_rx[:, 8:9]
    normed = (arrived[...].astype(jnp.float32) * scale * gain[:, own_columns]).astype(jnp.bfloat16)

    def pack(x, group):
        spot = pl.ds(pl.multiple_of((2 * x + group) * cap, cap), cap)
        return jnp.dot(placer[spot, :], normed, preferred_element_type=jnp.float32).astype(jnp.bfloat16)

    packed[0] = pack(other, g)
    cross = send(packed.at[0], rows(recv, z, xl), first_send.at[0], dispatch_recv.at[z, xl], at(other, z))
    cross.start()
    packed[1] = pack(xl, 1 - g)
    ext_own = send(packed.at[1], rows(recv, z, xl), first_send.at[3], dispatch_recv.at[z, xl], at(xl, across))
    ext_own.start()
    packed[2] = pack(other, 1 - g)
    ext_other = send(packed.at[2], rows(recv, z, xl), first_send.at[4], dispatch_recv.at[z, xl], at(other, across))
    ext_other.start()
    recv[z, pl.ds(pl.multiple_of(xl * cap, cap), cap), :] = pack(xl, g)
    own_far = send(rows(recv, z, xl), rows(recv, z, xl), first_send.at[1], dispatch_recv.at[z, xl], at(xl, far))
    own_near = send(rows(recv, z, xl), rows(recv, z, xl), first_send.at[2], dispatch_recv.at[z, xl], at(xl, near))
    own_far.start()

    @pl.when(is_mid)
    def _():
        own_near.start()

    relay_far = send(rows(recv, z, other), rows(recv, z, other), first_send.at[5], dispatch_recv.at[z, other], at(xl, far))
    relay_near = send(rows(recv, z, other), rows(recv, z, other), first_send.at[6], dispatch_recv.at[z, other], at(xl, near))
    relay_far.wait_recv()
    relay_far.start()

    @pl.when(is_mid)
    def _():
        relay_near.start()

    gate_copy.wait()
    down_copy.wait()

    def source(t):
        from1, from3, from5, from6 = (t + 7) // 8, (t + 5) // 8, (t + 3) // 8, (t + 2) // 8
        offset = (
            (from1 - from3) * (t + mid)
            + (from3 - from5) * (mid - t - 1)
            + (from5 - from6) * (4 * mid - 3)
            + from6 * (t - 8)
        )
        return (z + nd * offset + 2 * Z) % Z

    def forward(t, zz, x):
        to_near = mid * ((t + 5) // 8 - (t + 3) // 8 + (t + 2) // 8)
        target = (z + nd * (2 * to_near - 1) + Z) % Z
        return send(rows(recv, zz, x), rows(recv, zz, x), forward_send.at[t, x], dispatch_recv.at[zz, x], at(xl, target))

    def forwards(t):
        return (t >= 1) & (is_mid | (t <= 2))

    ways = (0, 1)

    def beyond(way):
        return (d + 1 - 2 * way + n_dp) % n_dp

    def span(ref, t, q, start, count):
        return ref.at[t, pl.ds(pl.multiple_of(q * piece + start, half), count)]

    def half_copy(t, way):
        return send(
            span(sum_tx, t, (d + 2) % n_dp, way * half, half), sum_half.at[t, way],
            half_send.at[t, way], half_recv.at[t, way], (s, j, beyond(way)),
        )

    def sum_copy(t, way):
        return send(
            span(sum_tx, t, beyond(way), 0, piece), sum_rx.at[t, way],
            sum_send.at[t, way], sum_recv.at[t, way], (s, j, beyond(way)),
        )

    def hid_copy(t, way):
        own = span(hid, t, d, 0, piece)
        return send(own, own, hid_send.at[t, way], hid_recv.at[t, way], (s, j, beyond(way)))

    def relay_copy(t, way):
        passed = span(hid, t, beyond(1 - way), way * half, half)
        return send(passed, passed, relay_send.at[t, way], relay_recv.at[t, way], (s, j, beyond(way)))

    def leaf_copy(zz, x):
        return send(rows(ret_near, zz, x), rows(ret_near, zz, x), ret_send.at[zz, x], near_recv.at[zz, x], at(xl, far))

    def up_copy(zz, x):
        return send(rows(ret_near, zz, x), rows(ret_far, zz, x), ret_send.at[zz, x], far_recv.at[zz, x], at(xl, far))

    def down_chain(zz, x):
        return send(rows(ret_far, zz, x), rows(ret_far, zz, x), ret_send.at[zz, x], far_recv.at[zz, x], at(xl, near))

    own_expert = 2 * xl + g

    def home_copy(zz, x):
        return send(rows(ret_far, zz, x), fin.at[own_expert], ret_send.at[zz, x], fin_recv.at[own_expert], at(x, zz))

    def each_step(i, carry):
        @pl.when(i <= 7)
        def _():
            zz = source(i)
            for x in (xl, other):
                @pl.when(i >= 1)
                def _():
                    forward(i, zz, x).wait_recv()

                @pl.when(forwards(i))
                def _():
                    forward(i, zz, x).start()

            terms = lax.dot_general(
                recv[zz], gate_v[...], (((1,), (1,)), ((), ())), preferred_element_type=jnp.float32
            )
            own_sum[i % 2] = terms
            sum_tx[i] = terms.astype(jnp.bfloat16)
            for way in ways:
                half_copy(i, way).start()

        @pl.when((i >= 1) & (i <= 8))
        def _():
            t = i - 1
            mine = pl.ds(pl.multiple_of(d * piece, piece), piece)
            total = own_sum[t % 2, mine, :]
            for way in ways:
                sum_copy(t, way).wait_recv()
                total = total + sum_rx[t, way].astype(jnp.float32)
            hid[t, mine, :] = (total / (1.0 + jnp.exp(-total))).astype(jnp.bfloat16)
            for way in ways:
                hid_copy(t, way).start()

        @pl.when((i >= 2) & (i <= 9))
        def _():
            t = i - 2
            zz = source(t)
            for way in ways:
                relay_copy(t, way).wait_recv()
            term[zz] = jnp.dot(hid[t], down_v[...], preferred_element_type=jnp.float32)

            @pl.when(is_end & (t >= 3))
            def _():
                ret_near[zz] = term[zz].astype(jnp.bfloat16)
                for x in range(2):
                    leaf_copy(zz, x).start()

        @pl.when(i <= 7)
        def _():
            for way in ways:
                half_copy(i, way).wait_recv()
                joined = pl.ds(pl.multiple_of(beyond(way) * piece + way * half, half), half)
                sum_tx[i, joined, :] = (own_sum[i % 2, joined, :] + sum_half[i, way].astype(jnp.float32)).astype(jnp.bfloat16)
                sum_copy(i, way).start()

        @pl.when((i >= 1) & (i <= 8))
        def _():
            for way in ways:
                hid_copy(i - 1, way).wait_recv()
                relay_copy(i - 1, way).start()

        @pl.when(is_mid & (i >= 7) & (i <= 10))
        def _():
            u = i - 7
            zz = (z + nd * ((u // 2) * (2 * u - 1) - 3 - u) + Z) % Z
            for x in range(2):
                leaf_copy(zz, x).wait_recv()
                block = slice(x * cap, (x + 1) * cap)
                ret_near[zz, block] = (term[zz, block] + ret_near[zz, block].astype(jnp.float32)).astype(jnp.bfloat16)
                up_copy(zz, x).start()

        @pl.when(is_mid & (i >= 8) & (i <= 10))
        def _():
            v = i - 8
            zz = (z + nd * (2 + v - 3 * (v // 2)) + Z) % Z
            for x in range(2):
                down_chain(zz, x).wait_recv()
                block = slice(x * cap, (x + 1) * cap)
                ret_far[zz, block] = (term[zz, block] + ret_far[zz, block].astype(jnp.float32)).astype(jnp.bfloat16)
                down_chain(zz, x).start()

        @pl.when(i == 11)
        def _():
            for x in (other, xl):
                block = pl.ds(pl.multiple_of(x * cap, cap), cap)
                up_copy(z, x).wait_recv()
                ret_far[z, block, :] = (term[z, block, :] + ret_far[z, block, :].astype(jnp.float32)).astype(jnp.bfloat16)

                @pl.when(is_mid)
                def _():
                    leaf_copy(z, x).wait_recv()
                    ret_far[z, block, :] = (
                        ret_far[z, block, :].astype(jnp.float32) + ret_near[z, block, :].astype(jnp.float32)
                    ).astype(jnp.bfloat16)

                if x is other:
                    home_copy(z, other).start()
            fin[own_expert] = ret_far[z, pl.ds(pl.multiple_of(xl * cap, cap), cap), :]

        @pl.when(is_end & ((i == 9) | (i == 10)))
        def _():
            zz = (z + nd * (i - 8) + Z) % Z
            for x in range(2):
                up_copy(zz, x).wait_recv()
                block = slice(x * cap, (x + 1) * cap)
                ret_far[zz, block] = (term[zz, block] + ret_far[zz, block].astype(jnp.float32)).astype(jnp.bfloat16)
                home_copy(zz, x).start()

        return carry

    lax.fori_loop(0, 12, each_step, 0)

    for x, group in ((other, g), (xl, 1 - g), (other, 1 - g)):
        e = 2 * x + group
        send(fin.at[e], fin.at[e], ret_send.at[0, 0], fin_recv.at[e], at(other, z)).wait_recv()

    gate_value = 1.0 / (1.0 + jnp.exp(-jnp.sum(chosen[...] * stat_rx[...], axis=1, keepdims=True)))
    expert_out = jnp.dot(
        unplacer[...], fin[...].reshape(4 * cap, part), preferred_element_type=jnp.float32
    )
    out[...] = (arrived[...].astype(jnp.float32) + gate_value * expert_out).astype(jnp.bfloat16)

    raw_copy.wait_send()
    stat_copy.wait_send()
    for copy in (cross, own_far, ext_own, ext_other, relay_far):
        copy.wait_send()

    @pl.when(is_mid)
    def _():
        own_near.wait_send()
        relay_near.wait_send()

    def sent(t, carry):
        zz = source(t)

        @pl.when(forwards(t))
        def _():
            for x in range(2):
                forward(t, zz, x).wait_send()

        for way in ways:
            half_copy(t, way).wait_send()
            sum_copy(t, way).wait_send()
            hid_copy(t, way).wait_send()
            relay_copy(t, way).wait_send()

        @pl.when(t >= 1)
        def _():
            for x in range(2):
                leaf_copy(zz, x).wait_send()

        return carry

    lax.fori_loop(0, STEPS, sent, 0)
    home_copy(z, other).wait_send()


def local(tokens, modality, routes, norm_gain, router, gate_weight, down_weight):
    tok, width = tokens.shape[1:]
    n_pipe, n_dp = lax.axis_size("pipe"), lax.axis_size("dp")
    part = width // n_dp
    cap = 2 * tok // router.shape[2]
    hidden = gate_weight.shape[2]
    piece = 2 * cap // n_dp
    bf16, f32 = jnp.bfloat16, jnp.float32
    vmem = pl.BlockSpec(memory_space=pltpu.VMEM)
    anywhere = pl.BlockSpec(memory_space=pl.ANY)
    dma = pltpu.SemaphoreType.DMA
    result = pl.pallas_call(
        functools.partial(kernel, n_pipe, n_dp),
        out_shape=jax.ShapeDtypeStruct((tok, part), bf16),
        in_specs=[anywhere] * 7,
        out_specs=vmem,
        scratch_shapes=[
            pltpu.VMEM((1, tok), jnp.int32),
            pltpu.VMEM((1, tok), jnp.int32),
            pltpu.VMEM((1, width), f32),
            pltpu.VMEM((router.shape[0], router.shape[2], width), bf16),
            pltpu.VMEM((tok, width), bf16),
            pltpu.VMEM((tok, width), bf16),
            pltpu.VMEM((hidden, part), bf16),
            pltpu.VMEM((hidden, part), bf16),
            pltpu.VMEM((tok, part), bf16),
            pltpu.VMEM((tok, 128), f32),
            pltpu.VMEM((tok, 128), f32),
            pltpu.VMEM((4 * cap, tok), bf16),
            pltpu.VMEM((tok, 4 * cap), bf16),
            pltpu.VMEM((tok, 128), f32),
            pltpu.VMEM((3, cap, part), bf16),
            pltpu.VMEM((STEPS, 2 * cap, part), bf16),
            pltpu.VMEM((STEPS, 2 * cap, hidden), bf16),
            pltpu.VMEM((STEPS, 2, piece // 2, hidden), bf16),
            pltpu.VMEM((STEPS, 2, piece, hidden), bf16),
            pltpu.VMEM((2, 2 * cap, hidden), f32),
            pltpu.VMEM((STEPS, 2 * cap, hidden), bf16),
            pltpu.VMEM((STEPS, 2 * cap, part), f32),
            pltpu.VMEM((STEPS, 2 * cap, part), bf16),
            pltpu.VMEM((STEPS, 2 * cap, part), bf16),
            pltpu.VMEM((4, cap, part), bf16),
            dma((7,)),
            dma((2,)),
            dma((2,)),
            dma((7,)),
            dma((STEPS, 2)),
            dma((STEPS, 2)),
            dma((STEPS, 2)),
            dma((STEPS, 2)),
            dma((STEPS, 2)),
            dma((STEPS, 2)),
            dma((STEPS, 2)),
            dma((STEPS, 2)),
            dma((STEPS, 2)),
            dma((STEPS, 2)),
            dma((STEPS, 2)),
            dma((STEPS, 2)),
            dma((STEPS, 2)),
            dma((4,)),
        ],
        compiler_params=pltpu.CompilerParams(
            collective_id=0, has_side_effects=True, vmem_limit_bytes=60 * 1024 * 1024
        ),
    )(
        tokens[0],
        modality,
        routes.reshape(1, tok),
        norm_gain.reshape(1, width),
        jnp.transpose(router, (0, 2, 1)),
        jnp.transpose(gate_weight[0]),
        down_weight[0],
    )
    return result[None]


def solution(mesh):
    placed = (
        P("pipe", "expert", None),
        P("pipe", "expert"),
        P("pipe", "expert", None),
        P(),
        P(),
        P("pipe", "dp", "expert"),
        P("pipe", "expert", "dp"),
    )
    return jax.shard_map(
        local, mesh=mesh, in_specs=placed, out_specs=P("pipe", "expert", "dp"), check_vma=False
    )
```

```python
import functools

import jax
import jax.numpy as jnp
from jax import lax
from jax.experimental import pallas as pl
from jax.experimental.pallas import tpu as pltpu
from jax.sharding import PartitionSpec as P

MESH = pl.DeviceIdType.MESH
epsilon = 1e-06
Z = 8
STEPS = 8


def kernel(
    n_pipe, n_dp,
    tokens, modality_hbm, routes_hbm, gain_hbm, router_hbm, gate_hbm, down_hbm,
    out,
    modality, routes, gain, router, tok_v, normed_v, gate_v, down_v, arrived, stat_tx, stat_rx, placer, unplacer, chosen,
    packed, recv, sum_tx, sum_half, sum_rx, own_sum, hid, term, ret_tx, joint, own_rx, fin, summed,
    local_sem, pipe_send, pipe_recv, first_send, forward_send, dispatch_recv,
    half_send, half_recv, sum_send, sum_recv, hid_send, hid_recv, relay_send, relay_recv, ret_send, joint_recv, own_recv, fin_recv,
):
    tok = tok_v.shape[0]
    cap = recv.shape[1] // 2
    part = recv.shape[2]
    piece = sum_rx.shape[2]
    half = piece // 2
    s, j, d = lax.axis_index("pipe"), lax.axis_index("expert"), lax.axis_index("dp")
    xl, z = j // Z, j % Z
    g, p = z // 4, z % 4
    mid = ((p + 1) // 2) % 2
    nd = 2 * (p // 2) - 1
    near, far, far2 = (z + nd + Z) % Z, (z - nd + Z) % Z, (z - 2 * nd + Z) % Z
    entry = (z + nd * (1 + mid) + Z) % Z
    inner = (z + nd * (3 + mid) + Z) % Z
    other = 1 - xl
    is_mid = mid == 1
    is_end = mid == 0

    def at(x, zz):
        return (s, x * Z + zz, d)

    def send(src, dst, send_sem, recv_sem, device):
        return pltpu.make_async_remote_copy(
            src_ref=src, dst_ref=dst, send_sem=send_sem, recv_sem=recv_sem,
            device_id=device, device_id_type=MESH,
        )

    def rows(ref, zz, x):
        return ref.at[zz, pl.ds(pl.multiple_of(x * cap, cap), cap)]

    tok_copy = pltpu.make_async_copy(tokens, tok_v, local_sem.at[0])
    gate_copy = pltpu.make_async_copy(gate_hbm, gate_v, local_sem.at[1])
    down_copy = pltpu.make_async_copy(down_hbm, down_v, local_sem.at[2])
    small = [
        pltpu.make_async_copy(a, b, local_sem.at[3 + k])
        for k, (a, b) in enumerate(((modality_hbm, modality), (routes_hbm, routes), (gain_hbm, gain), (router_hbm, router)))
    ]
    for copy in small:
        copy.start()
    tok_copy.start()

    barrier = pltpu.get_barrier_semaphore()
    partners = [
        ((s + 1) % n_pipe, j, d),
        ((s + n_pipe - 1) % n_pipe, j, d),
        (s, j, (d + 1) % n_dp),
        (s, j, (d + n_dp - 1) % n_dp),
        at(other, z), at(xl, far), at(xl, far2),
    ]
    for steps in (1 + mid, 2 + 2 * mid, 3 - 6 * mid):
        partners += [at(x, (z + nd * steps + Z) % Z) for x in (xl, other)]
    for device in partners:
        pl.semaphore_signal(barrier, inc=1, device_id=device, device_id_type=MESH)

    @pl.when(is_mid)
    def _():
        pl.semaphore_signal(barrier, inc=1, device_id=at(xl, near), device_id_type=MESH)

    gate_copy.start()
    down_copy.start()
    for copy in small:
        copy.wait()

    route_row = routes[...]
    hits = (lax.broadcasted_iota(jnp.int32, (8, tok), 0) == route_row).astype(jnp.float32)
    before = (
        lax.broadcasted_iota(jnp.int32, (tok, tok), 0) < lax.broadcasted_iota(jnp.int32, (tok, tok), 1)
    ).astype(jnp.bfloat16)
    earlier = jnp.dot(hits.astype(jnp.bfloat16), before, preferred_element_type=jnp.float32)
    rank = jnp.sum(hits * earlier, axis=0, keepdims=True)
    slot_row = route_row.astype(jnp.float32) * cap + rank
    slots = lax.broadcasted_iota(jnp.int32, (4 * cap, tok), 0).astype(jnp.float32)
    placer[...] = (slots == slot_row).astype(jnp.bfloat16)
    slot_col = jnp.transpose(jnp.broadcast_to(slot_row, (tok, tok)))[:, 0:1]
    slots = lax.broadcasted_iota(jnp.int32, (tok, 4 * cap), 1).astype(jnp.float32)
    unplacer[...] = (slots == slot_col).astype(jnp.bfloat16)
    pick_row = (modality[...] * 4 + route_row).astype(jnp.float32)
    pick_col = jnp.transpose(jnp.broadcast_to(pick_row, (tok, tok)))[:, 0:1]
    lanes = lax.broadcasted_iota(jnp.int32, (tok, 128), 1).astype(jnp.float32)
    chosen[...] = (lanes == pick_col).astype(jnp.float32)

    pl.semaphore_wait(barrier, len(partners) + mid)

    following = ((s + 1) % n_pipe, j, d)
    own_columns = pl.ds(pl.multiple_of(d * part, part), part)
    raw_copy = send(tokens.at[:, own_columns], arrived, pipe_send.at[0], pipe_recv.at[0], following)
    raw_copy.start()

    stat_tx[...] = jnp.zeros_like(stat_tx)
    tok_copy.wait()

    def norm_rows(i, carry):
        block = pl.ds(pl.multiple_of(i * 16, 16), 16)
        x = tok_v[block, :].astype(jnp.float32)
        scale = lax.rsqrt(jnp.mean(x * x, axis=-1, keepdims=True) + epsilon)
        normed_v[block, :] = (x * scale * gain[...]).astype(jnp.bfloat16)
        stat_tx[block, 8:9] = scale
        return carry

    lax.fori_loop(0, tok // 16, norm_rows, 0)
    for kind in range(2):
        stat_tx[:, 4 * kind : 4 * kind + 4] = lax.dot_general(
            normed_v[...], router[kind], (((1,), (1,)), ((), ())), preferred_element_type=jnp.float32
        )
    stat_copy = send(stat_tx, stat_rx, pipe_send.at[1], pipe_recv.at[1], following)
    stat_copy.start()
    raw_copy.wait_recv()
    stat_copy.wait_recv()

    scale = stat_rx[:, 8:9]
    normed = (arrived[...].astype(jnp.float32) * scale * gain[:, own_columns]).astype(jnp.bfloat16)

    def pack(x, group):
        spot = pl.ds(pl.multiple_of((2 * x + group) * cap, cap), cap)
        return jnp.dot(placer[spot, :], normed, preferred_element_type=jnp.float32).astype(jnp.bfloat16)

    packed[0] = pack(other, g)
    cross = send(packed.at[0], rows(recv, z, xl), first_send.at[0], dispatch_recv.at[z, xl], at(other, z))
    cross.start()
    def spread(src, x, targets, first):
        return [
            send(src, rows(recv, z, xl), first_send.at[first + k], dispatch_recv.at[z, xl], at(x, target))
            for k, target in enumerate(targets)
        ]

    packed[1] = pack(xl, 1 - g)
    ext_own = spread(packed.at[1], xl, (entry, inner), 1)
    for copy in ext_own:
        copy.start()
    packed[2] = pack(other, 1 - g)
    ext_other = spread(packed.at[2], other, (entry, inner), 3)
    for copy in ext_other:
        copy.start()
    recv[z, pl.ds(pl.multiple_of(xl * cap, cap), cap), :] = pack(xl, g)

    def inside(x, first):
        block = rows(recv, z, x)
        return [
            send(block, block, first_send.at[first + k], dispatch_recv.at[z, x], at(xl, target))
            for k, target in enumerate((far, far2, near))
        ]

    own_sends, relay_sends = inside(xl, 5), inside(other, 8)

    def start_inside(copies):
        copies[0].start()
        copies[1].start()

        @pl.when(is_mid)
        def _():
            copies[2].start()

    start_inside(own_sends)
    relay_sends[0].wait_recv()
    start_inside(relay_sends)

    gate_copy.wait()
    down_copy.wait()

    def source(t):
        from1, from3, from4, from6, from7 = (t + 7) // 8, (t + 5) // 8, (t + 4) // 8, (t + 2) // 8, (t + 1) // 8
        at_end = (from1 - from3) * t - (from3 - from6) * t - (from6 - from7) * 2 - from7
        at_mid = -(from1 - from4) * (t + 1) + (from4 - from6) * (t - 2) + (from6 - from7) - from7
        return (z + nd * (mid * at_mid + (1 - mid) * at_end) + 2 * Z) % Z

    def forward(t, zz, x):
        target = mid * near + (1 - mid) * far
        return send(rows(recv, zz, x), rows(recv, zz, x), forward_send.at[t, x], dispatch_recv.at[zz, x], at(xl, target))

    def forwards(t):
        return (t >= 1) & (t <= 2 + mid)

    ways = (0, 1)

    def beyond(way):
        return (d + 1 - 2 * way + n_dp) % n_dp

    def span(ref, t, q, start, count):
        return ref.at[t, pl.ds(pl.multiple_of(q * piece + start, half), count)]

    def half_copy(t, way):
        return send(
            span(sum_tx, t, (d + 2) % n_dp, way * half, half), sum_half.at[t, way],
            half_send.at[t, way], half_recv.at[t, way], (s, j, beyond(way)),
        )

    def sum_copy(t, way):
        return send(
            span(sum_tx, t, beyond(way), 0, piece), sum_rx.at[t, way],
            sum_send.at[t, way], sum_recv.at[t, way], (s, j, beyond(way)),
        )

    def hid_copy(t, way):
        own = span(hid, t, d, 0, piece)
        return send(own, own, hid_send.at[t, way], hid_recv.at[t, way], (s, j, beyond(way)))

    def relay_copy(t, way):
        passed = span(hid, t, beyond(1 - way), way * half, half)
        return send(passed, passed, relay_send.at[t, way], relay_recv.at[t, way], (s, j, beyond(way)))

    own_expert = 2 * xl + g

    def joint_copy(zz, x):
        target = mid * near + (1 - mid) * far
        return send(rows(ret_tx, zz, x), rows(joint, zz, x), ret_send.at[zz, x], joint_recv.at[zz, x], at(xl, target))

    def root_copy(zz, x, place, target):
        return send(rows(ret_tx, zz, x), rows(own_rx, place, x), ret_send.at[zz, x], own_recv.at[place, x], at(xl, target))

    def home_copy(zz, x, place):
        return send(rows(ret_tx, zz, x), fin.at[own_expert, place], ret_send.at[zz, x], fin_recv.at[own_expert, place], at(x, zz))

    def each_step(i, carry):
        @pl.when(i <= 7)
        def _():
            zz = source(i)
            for x in (xl, other):
                @pl.when(i >= 1)
                def _():
                    forward(i, zz, x).wait_recv()

                @pl.when(forwards(i))
                def _():
                    forward(i, zz, x).start()

            terms = lax.dot_general(
                recv[zz], gate_v[...], (((1,), (1,)), ((), ())), preferred_element_type=jnp.float32
            )
            own_sum[i % 4] = terms
            sum_tx[i] = terms.astype(jnp.bfloat16)
            for way in ways:
                half_copy(i, way).start()

        @pl.when((i >= 1) & (i <= 8))
        def _():
            t = i - 1
            for way in ways:
                half_copy(t, way).wait_recv()
                joined = pl.ds(pl.multiple_of(beyond(way) * piece + way * half, half), half)
                sum_tx[t, joined, :] = (own_sum[t % 4, joined, :] + sum_half[t, way].astype(jnp.float32)).astype(jnp.bfloat16)
                sum_copy(t, way).start()

        @pl.when((i >= 2) & (i <= 9))
        def _():
            t = i - 2
            mine = pl.ds(pl.multiple_of(d * piece, piece), piece)
            total = own_sum[t % 4, mine, :]
            for way in ways:
                sum_copy(t, way).wait_recv()
                total = total + sum_rx[t, way].astype(jnp.float32)
            hid[t, mine, :] = (total / (1.0 + jnp.exp(-total))).astype(jnp.bfloat16)
            for way in ways:
                hid_copy(t, way).start()

        @pl.when((i >= 3) & (i <= 10))
        def _():
            for way in ways:
                hid_copy(i - 3, way).wait_recv()
                relay_copy(i - 3, way).start()

        @pl.when(i >= 4)
        def _():
            t = i - 4
            zz = source(t)
            for way in ways:
                relay_copy(t, way).wait_recv()
            term[zz] = jnp.dot(hid[t], down_v[...], preferred_element_type=jnp.float32)

            @pl.when(t >= 3 + mid)
            def _():
                ret_tx[zz] = term[zz].astype(jnp.bfloat16)

            for x in range(2):
                @pl.when((t >= 3 + mid) & (t <= 5))
                def _():
                    joint_copy(zz, x).start()

                @pl.when(t == 6)
                def _():
                    root_copy(zz, x, 2 - mid, mid * near + (1 - mid) * far2).start()

                @pl.when(t == 7)
                def _():
                    root_copy(zz, x, mid, far).start()

        @pl.when((i >= 9 - mid) & (i <= 10))
        def _():
            zz = (z + nd * (mid * (6 - i) + (1 - mid) * (i - 8)) + 2 * Z) % Z
            for x in range(2):
                block = slice(x * cap, (x + 1) * cap)
                joint_copy(zz, x).wait_recv()
                ret_tx[zz, block] = (term[zz, block] + joint[zz, block].astype(jnp.float32)).astype(jnp.bfloat16)

                @pl.when(i == 8)
                def _():
                    root_copy(zz, x, 2, far2).start()

                @pl.when(i >= 9)
                def _():
                    home_copy(zz, x, mid).start()

        return carry

    lax.fori_loop(0, 12, each_step, 0)

    for x in (other, xl):
        block = pl.ds(pl.multiple_of(x * cap, cap), cap)
        for place in (1, 2):
            root_copy(z, x, place, far).wait_recv()
        ret_tx[z, block, :] = (
            term[z, block, :] + own_rx[1, block, :].astype(jnp.float32) + own_rx[2, block, :].astype(jnp.float32)
        ).astype(jnp.bfloat16)

        @pl.when(is_mid)
        def _():
            root_copy(z, x, 0, near).wait_recv()
            ret_tx[z, block, :] = (
                term[z, block, :] + own_rx[0, block, :].astype(jnp.float32)
                + own_rx[1, block, :].astype(jnp.float32) + own_rx[2, block, :].astype(jnp.float32)
            ).astype(jnp.bfloat16)

        if x is other:
            home_copy(z, other, 0).start()
    summed[pl.ds(pl.multiple_of(own_expert * cap, cap), cap), :] = ret_tx[z, pl.ds(pl.multiple_of(xl * cap, cap), cap), :]

    def arrival(e, place):
        return send(fin.at[e, place], fin.at[e, place], ret_send.at[0, 0], fin_recv.at[e, place], at(other, z))

    for x in (xl, other):
        e = 2 * x + 1 - g
        for place in range(2):
            arrival(e, place).wait_recv()
        summed[pl.ds(pl.multiple_of(e * cap, cap), cap), :] = (
            fin[e, 0].astype(jnp.float32) + fin[e, 1].astype(jnp.float32)
        ).astype(jnp.bfloat16)
    e = 2 * other + g
    arrival(e, 0).wait_recv()
    summed[pl.ds(pl.multiple_of(e * cap, cap), cap), :] = fin[e, 0]

    gate_value = 1.0 / (1.0 + jnp.exp(-jnp.sum(chosen[...] * stat_rx[...], axis=1, keepdims=True)))
    expert_out = jnp.dot(
        unplacer[...], summed[...], preferred_element_type=jnp.float32
    )
    out[...] = (arrived[...].astype(jnp.float32) + gate_value * expert_out).astype(jnp.bfloat16)

    raw_copy.wait_send()
    stat_copy.wait_send()
    for copy in [cross] + ext_own + ext_other + own_sends[:2] + relay_sends[:2]:
        copy.wait_send()

    @pl.when(is_mid)
    def _():
        own_sends[2].wait_send()
        relay_sends[2].wait_send()

    def sent(t, carry):
        zz = source(t)

        @pl.when(forwards(t))
        def _():
            for x in range(2):
                forward(t, zz, x).wait_send()

        for way in ways:
            half_copy(t, way).wait_send()
            sum_copy(t, way).wait_send()
            hid_copy(t, way).wait_send()
            relay_copy(t, way).wait_send()

        @pl.when(t >= 1)
        def _():
            for x in range(2):
                joint_copy(zz, x).wait_send()

        return carry

    lax.fori_loop(0, STEPS, sent, 0)
    home_copy(z, other, 0).wait_send()


def local(tokens, modality, routes, norm_gain, router, gate_weight, down_weight):
    tok, width = tokens.shape[1:]
    n_pipe, n_dp = lax.axis_size("pipe"), lax.axis_size("dp")
    part = width // n_dp
    cap = 2 * tok // router.shape[2]
    hidden = gate_weight.shape[2]
    piece = 2 * cap // n_dp
    bf16, f32 = jnp.bfloat16, jnp.float32
    vmem = pl.BlockSpec(memory_space=pltpu.VMEM)
    anywhere = pl.BlockSpec(memory_space=pl.ANY)
    dma = pltpu.SemaphoreType.DMA
    result = pl.pallas_call(
        functools.partial(kernel, n_pipe, n_dp),
        out_shape=jax.ShapeDtypeStruct((tok, part), bf16),
        in_specs=[anywhere] * 7,
        out_specs=vmem,
        scratch_shapes=[
            pltpu.VMEM((1, tok), jnp.int32),
            pltpu.VMEM((1, tok), jnp.int32),
            pltpu.VMEM((1, width), f32),
            pltpu.VMEM((router.shape[0], router.shape[2], width), bf16),
            pltpu.VMEM((tok, width), bf16),
            pltpu.VMEM((tok, width), bf16),
            pltpu.VMEM((hidden, part), bf16),
            pltpu.VMEM((hidden, part), bf16),
            pltpu.VMEM((tok, part), bf16),
            pltpu.VMEM((tok, 128), f32),
            pltpu.VMEM((tok, 128), f32),
            pltpu.VMEM((4 * cap, tok), bf16),
            pltpu.VMEM((tok, 4 * cap), bf16),
            pltpu.VMEM((tok, 128), f32),
            pltpu.VMEM((3, cap, part), bf16),
            pltpu.VMEM((STEPS, 2 * cap, part), bf16),
            pltpu.VMEM((STEPS, 2 * cap, hidden), bf16),
            pltpu.VMEM((STEPS, 2, piece // 2, hidden), bf16),
            pltpu.VMEM((STEPS, 2, piece, hidden), bf16),
            pltpu.VMEM((4, 2 * cap, hidden), f32),
            pltpu.VMEM((STEPS, 2 * cap, hidden), bf16),
            pltpu.VMEM((STEPS, 2 * cap, part), f32),
            pltpu.VMEM((STEPS, 2 * cap, part), bf16),
            pltpu.VMEM((STEPS, 2 * cap, part), bf16),
            pltpu.VMEM((3, 2 * cap, part), bf16),
            pltpu.VMEM((4, 2, cap, part), bf16),
            pltpu.VMEM((4 * cap, part), bf16),
            dma((7,)),
            dma((2,)),
            dma((2,)),
            dma((11,)),
            dma((STEPS, 2)),
            dma((STEPS, 2)),
            dma((STEPS, 2)),
            dma((STEPS, 2)),
            dma((STEPS, 2)),
            dma((STEPS, 2)),
            dma((STEPS, 2)),
            dma((STEPS, 2)),
            dma((STEPS, 2)),
            dma((STEPS, 2)),
            dma((STEPS, 2)),
            dma((STEPS, 2)),
            dma((3, 2)),
            dma((4, 2)),
        ],
        compiler_params=pltpu.CompilerParams(
            collective_id=0, has_side_effects=True, vmem_limit_bytes=60 * 1024 * 1024
        ),
    )(
        tokens[0],
        modality,
        routes.reshape(1, tok),
        norm_gain.reshape(1, width),
        jnp.transpose(router, (0, 2, 1)),
        jnp.transpose(gate_weight[0]),
        down_weight[0],
    )
    return result[None]


def solution(mesh):
    placed = (
        P("pipe", "expert", None),
        P("pipe", "expert"),
        P("pipe", "expert", None),
        P(),
        P(),
        P("pipe", "dp", "expert"),
        P("pipe", "expert", "dp"),
    )
    return jax.shard_map(
        local, mesh=mesh, in_specs=placed, out_specs=P("pipe", "expert", "dp"), check_vma=False
    )
```

```python
import functools

import jax
import jax.numpy as jnp
from jax import lax
from jax.experimental import pallas as pl
from jax.experimental.pallas import tpu as pltpu
from jax.sharding import PartitionSpec as P

MESH = pl.DeviceIdType.MESH
epsilon = 1e-06
Z = 8
STEPS = 8


def kernel(
    n_pipe, n_dp,
    tokens, modality_hbm, routes_hbm, gain_hbm, router_hbm, gate_hbm, down_hbm,
    out,
    modality, routes, gain, router, tok_v, normed_v, gate_v, down_v, arrived, stat_tx, stat_rx, placer, unplacer, chosen,
    packed, recv, sum_tx, sum_rx, own_sum, hid, term, ret_tx, joint, own_rx, fin, summed,
    local_sem, pipe_send, pipe_recv, first_send, forward_send, dispatch_recv,
    sum_send, sum_recv, hid_send, hid_recv, ret_send, joint_recv, own_recv, fin_recv,
):
    tok = tok_v.shape[0]
    cap = recv.shape[1] // 2
    part = recv.shape[2]
    piece = sum_rx.shape[2]
    s, j, d = lax.axis_index("pipe"), lax.axis_index("expert"), lax.axis_index("dp")
    xl, z = j // Z, j % Z
    g, p = z // 4, z % 4
    mid = ((p + 1) // 2) % 2
    nd = 2 * (p // 2) - 1
    near, far = (z + nd + Z) % Z, (z - nd + Z) % Z
    entry = (z + nd * (1 + mid) + Z) % Z
    other = 1 - xl
    is_mid = mid == 1
    is_end = mid == 0

    def at(x, zz):
        return (s, x * Z + zz, d)

    def send(src, dst, send_sem, recv_sem, device):
        return pltpu.make_async_remote_copy(
            src_ref=src, dst_ref=dst, send_sem=send_sem, recv_sem=recv_sem,
            device_id=device, device_id_type=MESH,
        )

    def rows(ref, zz, x):
        return ref.at[zz, pl.ds(pl.multiple_of(x * cap, cap), cap)]

    tok_copy = pltpu.make_async_copy(tokens, tok_v, local_sem.at[0])
    gate_copy = pltpu.make_async_copy(gate_hbm, gate_v, local_sem.at[1])
    down_copy = pltpu.make_async_copy(down_hbm, down_v, local_sem.at[2])
    small = [
        pltpu.make_async_copy(a, b, local_sem.at[3 + k])
        for k, (a, b) in enumerate(((modality_hbm, modality), (routes_hbm, routes), (gain_hbm, gain), (router_hbm, router)))
    ]
    for copy in small:
        copy.start()
    tok_copy.start()

    barrier = pltpu.get_barrier_semaphore()
    partners = [
        ((s + 1) % n_pipe, j, d),
        ((s + n_pipe - 1) % n_pipe, j, d),
        at(other, z), at(xl, far),
    ] + [(s, j, (d + k) % n_dp) for k in range(1, n_dp)]
    for steps in (1 + 2 * mid, 2):
        partners += [at(x, (z + nd * steps + Z) % Z) for x in (xl, other)]
    for device in partners:
        pl.semaphore_signal(barrier, inc=1, device_id=device, device_id_type=MESH)

    @pl.when(is_mid)
    def _():
        pl.semaphore_signal(barrier, inc=1, device_id=at(xl, near), device_id_type=MESH)

    gate_copy.start()
    down_copy.start()
    for copy in small:
        copy.wait()

    route_row = routes[...]
    hits = (lax.broadcasted_iota(jnp.int32, (8, tok), 0) == route_row).astype(jnp.float32)
    before = (
        lax.broadcasted_iota(jnp.int32, (tok, tok), 0) < lax.broadcasted_iota(jnp.int32, (tok, tok), 1)
    ).astype(jnp.bfloat16)
    earlier = jnp.dot(hits.astype(jnp.bfloat16), before, preferred_element_type=jnp.float32)
    rank = jnp.sum(hits * earlier, axis=0, keepdims=True)
    slot_row = route_row.astype(jnp.float32) * cap + rank
    slots = lax.broadcasted_iota(jnp.int32, (4 * cap, tok), 0).astype(jnp.float32)
    placer[...] = (slots == slot_row).astype(jnp.bfloat16)
    slot_col = jnp.transpose(jnp.broadcast_to(slot_row, (tok, tok)))[:, 0:1]
    slots = lax.broadcasted_iota(jnp.int32, (tok, 4 * cap), 1).astype(jnp.float32)
    unplacer[...] = (slots == slot_col).astype(jnp.bfloat16)
    pick_row = (modality[...] * 4 + route_row).astype(jnp.float32)
    pick_col = jnp.transpose(jnp.broadcast_to(pick_row, (tok, tok)))[:, 0:1]
    lanes = lax.broadcasted_iota(jnp.int32, (tok, 128), 1).astype(jnp.float32)
    chosen[...] = (lanes == pick_col).astype(jnp.float32)

    pl.semaphore_wait(barrier, len(partners) + mid)

    following = ((s + 1) % n_pipe, j, d)
    own_columns = pl.ds(pl.multiple_of(d * part, part), part)
    raw_copy = send(tokens.at[:, own_columns], arrived, pipe_send.at[0], pipe_recv.at[0], following)
    raw_copy.start()

    stat_tx[...] = jnp.zeros_like(stat_tx)
    tok_copy.wait()

    def norm_rows(i, carry):
        block = pl.ds(pl.multiple_of(i * 16, 16), 16)
        x = tok_v[block, :].astype(jnp.float32)
        scale = lax.rsqrt(jnp.mean(x * x, axis=-1, keepdims=True) + epsilon)
        normed_v[block, :] = (x * scale * gain[...]).astype(jnp.bfloat16)
        stat_tx[block, 8:9] = scale
        return carry

    lax.fori_loop(0, tok // 16, norm_rows, 0)
    for kind in range(2):
        stat_tx[:, 4 * kind : 4 * kind + 4] = lax.dot_general(
            normed_v[...], router[kind], (((1,), (1,)), ((), ())), preferred_element_type=jnp.float32
        )
    stat_copy = send(stat_tx, stat_rx, pipe_send.at[1], pipe_recv.at[1], following)
    stat_copy.start()
    raw_copy.wait_recv()
    stat_copy.wait_recv()

    scale = stat_rx[:, 8:9]
    normed = (arrived[...].astype(jnp.float32) * scale * gain[:, own_columns]).astype(jnp.bfloat16)

    def pack(x, group):
        spot = pl.ds(pl.multiple_of((2 * x + group) * cap, cap), cap)
        return jnp.dot(placer[spot, :], normed, preferred_element_type=jnp.float32).astype(jnp.bfloat16)

    packed[0] = pack(other, g)
    cross = send(packed.at[0], rows(recv, z, xl), first_send.at[0], dispatch_recv.at[z, xl], at(other, z))
    cross.start()
    packed[1] = pack(xl, 1 - g)
    ext_own = send(packed.at[1], rows(recv, z, xl), first_send.at[1], dispatch_recv.at[z, xl], at(xl, entry))
    ext_own.start()
    recv[z, pl.ds(pl.multiple_of(xl * cap, cap), cap), :] = pack(xl, g)

    def inside(x, first):
        block = rows(recv, z, x)
        return [
            send(block, block, first_send.at[first + k], dispatch_recv.at[z, x], at(xl, target))
            for k, target in enumerate((far, near))
        ]

    own_sends, relay_sends = inside(xl, 3), inside(other, 5)

    def start_inside(copies):
        copies[0].start()

        @pl.when(is_mid)
        def _():
            copies[1].start()

    start_inside(own_sends)
    packed[2] = pack(other, 1 - g)
    ext_other = send(packed.at[2], rows(recv, z, xl), first_send.at[2], dispatch_recv.at[z, xl], at(other, entry))
    ext_other.start()
    relay_sends[0].wait_recv()
    start_inside(relay_sends)

    gate_copy.wait()
    down_copy.wait()

    def source(t):
        at_mid = (t % 2) * ((t + 1) // 2) - (1 - t % 2) * (t // 2)
        at_end = sum(
            offset * (1 - ((t - k) * (t - k) + 48) // 49) for k, offset in enumerate((0, -1, 1, -2, -3, 2, -4, -5))
        )
        return (z + nd * (mid * at_mid + (1 - mid) * at_end) + 2 * Z) % Z

    def passed_on(t):
        return (z + nd * ((t + 1) // 2) + Z) % Z

    def forward(t, zz, x):
        to_near = mid * (1 - (t % 2) * (1 - t // 7))
        target = (z + nd * (2 * to_near - 1) + Z) % Z
        return send(rows(recv, zz, x), rows(recv, zz, x), forward_send.at[t, x], dispatch_recv.at[zz, x], at(xl, target))

    def end_forwards(t):
        return is_end & ((t == 1) | (t == 3))

    def span(ref, t, q):
        return ref.at[t, pl.ds(pl.multiple_of(q * piece, piece), piece)]

    def sum_copy(t, k):
        q = (d + k) % n_dp
        return send(span(sum_tx, t, q), sum_rx.at[t, k - 1], sum_send.at[t, k - 1], sum_recv.at[t, k - 1], (s, j, q))

    def hid_copy(t, k):
        own = span(hid, t, d)
        return send(own, own, hid_send.at[t, k - 1], hid_recv.at[t, k - 1], (s, j, (d + k) % n_dp))

    own_expert = 2 * xl + g

    def joint_copy(zz, x, target):
        return send(rows(ret_tx, zz, x), rows(joint, zz, x), ret_send.at[zz, x], joint_recv.at[zz, x], at(xl, target))

    def root_copy(zz, x, place, target):
        return send(rows(ret_tx, zz, x), rows(own_rx, place, x), ret_send.at[zz, x], own_recv.at[place, x], at(xl, target))

    def home_copy(zz, x, place):
        return send(rows(ret_tx, zz, x), fin.at[own_expert, place], ret_send.at[zz, x], fin_recv.at[own_expert, place], at(x, zz))

    def each_step(i, carry):
        @pl.when(i <= 7)
        def _():
            @pl.when(end_forwards(i))
            def _():
                for x in (xl, other):
                    forward(i, passed_on(i), x).wait_recv()
                    forward(i, passed_on(i), x).start()

            zz = source(i)
            for x in (xl, other):
                @pl.when((i >= 1) & (is_mid | ((i != 2) & (i != 5))))
                def _():
                    forward(i, zz, x).wait_recv()

                @pl.when((i >= 1) & is_mid)
                def _():
                    forward(i, zz, x).start()

            terms = lax.dot_general(
                gate_v[...], recv[zz], (((1,), (1,)), ((), ())), preferred_element_type=jnp.float32
            )
            own_sum[i % 4] = terms
            sum_tx[i] = terms.astype(jnp.bfloat16)
            for k in range(1, n_dp):
                sum_copy(i, k).start()

        @pl.when((i >= 1) & (i <= 8))
        def _():
            t = i - 1
            mine = pl.ds(pl.multiple_of(d * piece, piece), piece)
            total = own_sum[t % 4, mine, :]
            for k in range(1, n_dp):
                sum_copy(t, k).wait_recv()
                total = total + sum_rx[t, k - 1].astype(jnp.float32)
            hid[t, mine, :] = (total / (1.0 + jnp.exp(-total))).astype(jnp.bfloat16)
            for k in range(1, n_dp):
                hid_copy(t, k).start()

        @pl.when((i >= 2) & (i <= 9))
        def _():
            t = i - 2
            zz = source(t)
            for k in range(1, n_dp):
                hid_copy(t, k).wait_recv()
            term[zz] = lax.dot_general(
                hid[t], down_v[...], (((0,), (0,)), ((), ())), preferred_element_type=jnp.float32
            )

            @pl.when(is_end & (t >= 1))
            def _():
                ret_tx[zz] = term[zz].astype(jnp.bfloat16)

            for x in range(2):
                @pl.when(is_end & ((t == 2) | (t == 5)))
                def _():
                    home_copy(zz, x, 0).start()

                @pl.when(is_end & (t == 1))
                def _():
                    root_copy(zz, x, 0, far).start()

                @pl.when(is_end & ((t == 3) | (t == 4) | (t >= 6)))
                def _():
                    joint_copy(zz, x, far).start()

        def join(zz, x):
            block = slice(x * cap, (x + 1) * cap)
            joint_copy(zz, x, far).wait_recv()
            ret_tx[zz, block] = (term[zz, block] + joint[zz, block].astype(jnp.float32)).astype(jnp.bfloat16)

        @pl.when(is_mid & (i >= 6) & (i <= 10) & (i != 8))
        def _():
            u = i - 6
            zz = (z + nd * (u // 3 - u - 1) + Z) % Z
            for x in range(2):
                join(zz, x)

                @pl.when(i == 6)
                def _():
                    root_copy(zz, x, 1, far).start()

                @pl.when(i >= 7)
                def _():
                    joint_copy(zz, x, far).start()

        @pl.when(is_mid & ((i == 8) | (i >= 10)))
        def _():
            v = i - 8
            zz = (z + nd * (1 + v - v // 2) + Z) % Z
            for x in range(2):
                join(zz, x)

                @pl.when(i == 8)
                def _():
                    root_copy(zz, x, 1, near).start()

                @pl.when(i >= 10)
                def _():
                    home_copy(zz, x, 1).start()

        @pl.when(i == 9 - mid)
        def _():
            for x in (other, xl):
                block = pl.ds(pl.multiple_of(x * cap, cap), cap)
                root_copy(z, x, 1, far).wait_recv()
                total = term[z, block, :] + own_rx[1, block, :].astype(jnp.float32)

                @pl.when(is_end)
                def _():
                    ret_tx[z, block, :] = total.astype(jnp.bfloat16)

                @pl.when(is_mid)
                def _():
                    root_copy(z, x, 0, near).wait_recv()
                    ret_tx[z, block, :] = (total + own_rx[0, block, :].astype(jnp.float32)).astype(jnp.bfloat16)

                if x is other:
                    home_copy(z, other, 0).start()

        return carry

    lax.fori_loop(0, 12, each_step, 0)

    summed[pl.ds(pl.multiple_of(own_expert * cap, cap), cap), :] = ret_tx[z, pl.ds(pl.multiple_of(xl * cap, cap), cap), :]

    def arrival(e, place):
        return send(fin.at[e, place], fin.at[e, place], ret_send.at[0, 0], fin_recv.at[e, place], at(other, z))

    for x in (xl, other):
        e = 2 * x + 1 - g
        for place in range(2):
            arrival(e, place).wait_recv()
        summed[pl.ds(pl.multiple_of(e * cap, cap), cap), :] = (
            fin[e, 0].astype(jnp.float32) + fin[e, 1].astype(jnp.float32)
        ).astype(jnp.bfloat16)
    e = 2 * other + g
    arrival(e, 0).wait_recv()
    summed[pl.ds(pl.multiple_of(e * cap, cap), cap), :] = fin[e, 0]

    gate_value = 1.0 / (1.0 + jnp.exp(-jnp.sum(chosen[...] * stat_rx[...], axis=1, keepdims=True)))
    expert_out = jnp.dot(
        unplacer[...], summed[...], preferred_element_type=jnp.float32
    )
    out[...] = (arrived[...].astype(jnp.float32) + gate_value * expert_out).astype(jnp.bfloat16)

    raw_copy.wait_send()
    stat_copy.wait_send()
    for copy in (cross, ext_own, ext_other, own_sends[0], relay_sends[0]):
        copy.wait_send()

    @pl.when(is_mid)
    def _():
        own_sends[1].wait_send()
        relay_sends[1].wait_send()

    def sent(t, carry):
        zz = source(t)

        @pl.when(end_forwards(t) | ((t >= 1) & is_mid))
        def _():
            for x in range(2):
                forward(t, zz, x).wait_send()

        for k in range(1, n_dp):
            sum_copy(t, k).wait_send()
            hid_copy(t, k).wait_send()

        @pl.when(t >= 1)
        def _():
            for x in range(2):
                joint_copy(zz, x, far).wait_send()

        return carry

    lax.fori_loop(0, STEPS, sent, 0)
    home_copy(z, other, 0).wait_send()


def local(tokens, modality, routes, norm_gain, router, gate_weight, down_weight):
    tok, width = tokens.shape[1:]
    n_pipe, n_dp = lax.axis_size("pipe"), lax.axis_size("dp")
    part = width // n_dp
    cap = 2 * tok // router.shape[2]
    hidden = gate_weight.shape[2]
    piece = hidden // n_dp
    bf16, f32 = jnp.bfloat16, jnp.float32
    vmem = pl.BlockSpec(memory_space=pltpu.VMEM)
    anywhere = pl.BlockSpec(memory_space=pl.ANY)
    dma = pltpu.SemaphoreType.DMA
    result = pl.pallas_call(
        functools.partial(kernel, n_pipe, n_dp),
        out_shape=jax.ShapeDtypeStruct((tok, part), bf16),
        in_specs=[anywhere] * 7,
        out_specs=vmem,
        scratch_shapes=[
            pltpu.VMEM((1, tok), jnp.int32),
            pltpu.VMEM((1, tok), jnp.int32),
            pltpu.VMEM((1, width), f32),
            pltpu.VMEM((router.shape[0], router.shape[2], width), bf16),
            pltpu.VMEM((tok, width), bf16),
            pltpu.VMEM((tok, width), bf16),
            pltpu.VMEM((hidden, part), bf16),
            pltpu.VMEM((hidden, part), bf16),
            pltpu.VMEM((tok, part), bf16),
            pltpu.VMEM((tok, 128), f32),
            pltpu.VMEM((tok, 128), f32),
            pltpu.VMEM((4 * cap, tok), bf16),
            pltpu.VMEM((tok, 4 * cap), bf16),
            pltpu.VMEM((tok, 128), f32),
            pltpu.VMEM((3, cap, part), bf16),
            pltpu.VMEM((STEPS, 2 * cap, part), bf16),
            pltpu.VMEM((STEPS, hidden, 2 * cap), bf16),
            pltpu.VMEM((STEPS, n_dp - 1, piece, 2 * cap), bf16),
            pltpu.VMEM((4, hidden, 2 * cap), f32),
            pltpu.VMEM((STEPS, hidden, 2 * cap), bf16),
            pltpu.VMEM((STEPS, 2 * cap, part), f32),
            pltpu.VMEM((STEPS, 2 * cap, part), bf16),
            pltpu.VMEM((STEPS, 2 * cap, part), bf16),
            pltpu.VMEM((2, 2 * cap, part), bf16),
            pltpu.VMEM((4, 2, cap, part), bf16),
            pltpu.VMEM((4 * cap, part), bf16),
            dma((7,)),
            dma((2,)),
            dma((2,)),
            dma((7,)),
            dma((STEPS, 2)),
            dma((STEPS, 2)),
            dma((STEPS, n_dp - 1)),
            dma((STEPS, n_dp - 1)),
            dma((STEPS, n_dp - 1)),
            dma((STEPS, n_dp - 1)),
            dma((STEPS, 2)),
            dma((STEPS, 2)),
            dma((2, 2)),
            dma((4, 2)),
        ],
        compiler_params=pltpu.CompilerParams(
            collective_id=0, has_side_effects=True, vmem_limit_bytes=60 * 1024 * 1024
        ),
    )(
        tokens[0],
        modality,
        routes.reshape(1, tok),
        norm_gain.reshape(1, width),
        jnp.transpose(router, (0, 2, 1)),
        jnp.transpose(gate_weight[0]),
        down_weight[0],
    )
    return result[None]


def solution(mesh):
    placed = (
        P("pipe", "expert", None),
        P("pipe", "expert"),
        P("pipe", "expert", None),
        P(),
        P(),
        P("pipe", "dp", "expert"),
        P("pipe", "expert", "dp"),
    )
    return jax.shard_map(
        local, mesh=mesh, in_specs=placed, out_specs=P("pipe", "expert", "dp"), check_vma=False
    )
```

```python
import functools

import jax
import jax.numpy as jnp
from jax import lax
from jax.experimental import pallas as pl
from jax.experimental.pallas import tpu as pltpu
from jax.sharding import PartitionSpec as P

MESH = pl.DeviceIdType.MESH
epsilon = 1e-06
Z = 8
STEPS = 8


def kernel(
    n_pipe, n_dp,
    tokens, modality_hbm, routes_hbm, gain_hbm, router_hbm, gate_hbm, down_hbm,
    out,
    modality, routes, gain, router, tok_v, normed_v, gate_v, down_v, arrived, stat_tx, stat_rx, placer, unplacer, chosen,
    packed, recv, sum_tx, sum_rx, own_sum, hid, term, ret_tx, joint, own_rx, fin, summed,
    local_sem, pipe_send, pipe_recv, first_send, forward_send, dispatch_recv,
    sum_send, sum_recv, hid_send, hid_recv, ret_send, joint_recv, own_recv, fin_recv,
):
    tok = tok_v.shape[0]
    cap = recv.shape[1] // 2
    part = recv.shape[2]
    piece = sum_rx.shape[2]
    s, j, d = lax.axis_index("pipe"), lax.axis_index("expert"), lax.axis_index("dp")
    xl, z = j // Z, j % Z
    g, p = z // 4, z % 4
    mid = ((p + 1) // 2) % 2
    nd = 2 * (p // 2) - 1
    near, far = (z + nd + Z) % Z, (z - nd + Z) % Z
    entry = (z + nd * (1 + mid) + Z) % Z
    other = 1 - xl
    is_mid = mid == 1
    is_end = mid == 0

    def at(x, zz):
        return (s, x * Z + zz, d)

    def send(src, dst, send_sem, recv_sem, device):
        return pltpu.make_async_remote_copy(
            src_ref=src, dst_ref=dst, send_sem=send_sem, recv_sem=recv_sem,
            device_id=device, device_id_type=MESH,
        )

    def rows(ref, zz, x):
        return ref.at[zz, pl.ds(pl.multiple_of(x * cap, cap), cap)]

    tok_copy = pltpu.make_async_copy(tokens, tok_v, local_sem.at[0])
    gate_copy = pltpu.make_async_copy(gate_hbm, gate_v, local_sem.at[1])
    down_copy = pltpu.make_async_copy(down_hbm, down_v, local_sem.at[2])
    small = [
        pltpu.make_async_copy(a, b, local_sem.at[3 + k])
        for k, (a, b) in enumerate(((modality_hbm, modality), (routes_hbm, routes), (gain_hbm, gain), (router_hbm, router)))
    ]
    for copy in small:
        copy.start()
    tok_copy.start()

    barrier = pltpu.get_barrier_semaphore()
    partners = [
        ((s + 1) % n_pipe, j, d),
        ((s + n_pipe - 1) % n_pipe, j, d),
        at(other, z), at(xl, far),
    ] + [(s, j, (d + k) % n_dp) for k in range(1, n_dp)]
    for steps in (1 + 2 * mid, 2):
        partners += [at(x, (z + nd * steps + Z) % Z) for x in (xl, other)]
    for device in partners:
        pl.semaphore_signal(barrier, inc=1, device_id=device, device_id_type=MESH)

    @pl.when(is_mid)
    def _():
        pl.semaphore_signal(barrier, inc=1, device_id=at(xl, near), device_id_type=MESH)

    gate_copy.start()
    down_copy.start()
    for copy in small:
        copy.wait()

    route_row = routes[...]
    hits = (lax.broadcasted_iota(jnp.int32, (8, tok), 0) == route_row).astype(jnp.float32)
    before = (
        lax.broadcasted_iota(jnp.int32, (tok, tok), 0) < lax.broadcasted_iota(jnp.int32, (tok, tok), 1)
    ).astype(jnp.bfloat16)
    earlier = jnp.dot(hits.astype(jnp.bfloat16), before, preferred_element_type=jnp.float32)
    rank = jnp.sum(hits * earlier, axis=0, keepdims=True)
    slot_row = route_row.astype(jnp.float32) * cap + rank
    slots = lax.broadcasted_iota(jnp.int32, (4 * cap, tok), 0).astype(jnp.float32)
    placer[...] = (slots == slot_row).astype(jnp.bfloat16)
    slot_col = jnp.transpose(jnp.broadcast_to(slot_row, (tok, tok)))[:, 0:1]
    slots = lax.broadcasted_iota(jnp.int32, (tok, 4 * cap), 1).astype(jnp.float32)
    unplacer[...] = (slots == slot_col).astype(jnp.bfloat16)
    pick_row = (modality[...] * 4 + route_row).astype(jnp.float32)
    pick_col = jnp.transpose(jnp.broadcast_to(pick_row, (tok, tok)))[:, 0:1]
    lanes = lax.broadcasted_iota(jnp.int32, (tok, 128), 1).astype(jnp.float32)
    chosen[...] = (lanes == pick_col).astype(jnp.float32)

    pl.semaphore_wait(barrier, len(partners) + mid)

    following = ((s + 1) % n_pipe, j, d)
    own_columns = pl.ds(pl.multiple_of(d * part, part), part)
    raw_copy = send(tokens.at[:, own_columns], arrived, pipe_send.at[0], pipe_recv.at[0], following)
    raw_copy.start()

    stat_tx[...] = jnp.zeros_like(stat_tx)
    tok_copy.wait()

    def norm_rows(i, carry):
        block = pl.ds(pl.multiple_of(i * 16, 16), 16)
        x = tok_v[block, :].astype(jnp.float32)
        scale = lax.rsqrt(jnp.mean(x * x, axis=-1, keepdims=True) + epsilon)
        normed_v[block, :] = (x * scale * gain[...]).astype(jnp.bfloat16)
        stat_tx[block, 8:9] = scale
        return carry

    lax.fori_loop(0, tok // 16, norm_rows, 0)
    for kind in range(2):
        stat_tx[:, 4 * kind : 4 * kind + 4] = lax.dot_general(
            normed_v[...], router[kind], (((1,), (1,)), ((), ())), preferred_element_type=jnp.float32
        )
    stat_copy = send(stat_tx, stat_rx, pipe_send.at[1], pipe_recv.at[1], following)
    stat_copy.start()
    raw_copy.wait_recv()
    stat_copy.wait_recv()

    scale = stat_rx[:, 8:9]
    normed = (arrived[...].astype(jnp.float32) * scale * gain[:, own_columns]).astype(jnp.bfloat16)

    def pack(x, group):
        spot = pl.ds(pl.multiple_of((2 * x + group) * cap, cap), cap)
        return jnp.dot(placer[spot, :], normed, preferred_element_type=jnp.float32).astype(jnp.bfloat16)

    packed[0] = pack(other, g)
    cross = send(packed.at[0], rows(recv, z, xl), first_send.at[0], dispatch_recv.at[z, xl], at(other, z))
    cross.start()
    packed[1] = pack(xl, 1 - g)
    ext_own = send(packed.at[1], rows(recv, z, xl), first_send.at[1], dispatch_recv.at[z, xl], at(xl, entry))
    ext_own.start()
    packed[2] = pack(other, 1 - g)
    ext_other = send(packed.at[2], rows(recv, z, xl), first_send.at[2], dispatch_recv.at[z, xl], at(other, entry))
    ext_other.start()
    recv[z, pl.ds(pl.multiple_of(xl * cap, cap), cap), :] = pack(xl, g)

    def inside(x, first):
        block = rows(recv, z, x)
        return [
            send(block, block, first_send.at[first + k], dispatch_recv.at[z, x], at(xl, target))
            for k, target in enumerate((far, near))
        ]

    own_sends, relay_sends = inside(xl, 3), inside(other, 5)

    def start_inside(copies):
        copies[0].start()

        @pl.when(is_mid)
        def _():
            copies[1].start()

    start_inside(own_sends)
    relay_sends[0].wait_recv()
    start_inside(relay_sends)

    gate_copy.wait()
    down_copy.wait()

    def source(t):
        at_mid = (t % 2) * ((t + 1) // 2) - (1 - t % 2) * (t // 2)
        at_end = sum(
            offset * (1 - ((t - k) * (t - k) + 48) // 49) for k, offset in enumerate((0, -1, 1, -2, -3, 2, -4, -5))
        )
        return (z + nd * (mid * at_mid + (1 - mid) * at_end) + 2 * Z) % Z

    def passed_on(t):
        return (z + nd * ((t + 1) // 2) + Z) % Z

    def forward(t, zz, x):
        to_near = mid * (1 - (t % 2) * (1 - t // 7))
        target = (z + nd * (2 * to_near - 1) + Z) % Z
        return send(rows(recv, zz, x), rows(recv, zz, x), forward_send.at[t, x], dispatch_recv.at[zz, x], at(xl, target))

    def end_forwards(t):
        return is_end & ((t == 1) | (t == 3))

    def span(ref, t, q):
        return ref.at[t, pl.ds(pl.multiple_of(q * piece, piece), piece)]

    def sum_copy(t, k):
        q = (d + k) % n_dp
        return send(span(sum_tx, t, q), sum_rx.at[t, k - 1], sum_send.at[t, k - 1], sum_recv.at[t, k - 1], (s, j, q))

    def hid_copy(t, k):
        own = span(hid, t, d)
        return send(own, own, hid_send.at[t, k - 1], hid_recv.at[t, k - 1], (s, j, (d + k) % n_dp))

    own_expert = 2 * xl + g

    def joint_copy(zz, x, target):
        return send(rows(ret_tx, zz, x), rows(joint, zz, x), ret_send.at[zz, x], joint_recv.at[zz, x], at(xl, target))

    def root_copy(zz, x, place, target):
        return send(rows(ret_tx, zz, x), rows(own_rx, place, x), ret_send.at[zz, x], own_recv.at[place, x], at(xl, target))

    def home_copy(zz, x, place):
        return send(rows(ret_tx, zz, x), fin.at[own_expert, place], ret_send.at[zz, x], fin_recv.at[own_expert, place], at(x, zz))

    def each_step(i, carry):
        @pl.when(i <= 7)
        def _():
            @pl.when(end_forwards(i))
            def _():
                for x in (xl, other):
                    forward(i, passed_on(i), x).wait_recv()
                    forward(i, passed_on(i), x).start()

            zz = source(i)
            for x in (xl, other):
                @pl.when(is_end & (i >= 1) & (i != 2) & (i != 5))
                def _():
                    forward(i, zz, x).wait_recv()

            terms = lax.dot_general(
                gate_v[...], recv[zz], (((1,), (1,)), ((), ())), preferred_element_type=jnp.float32
            )
            own_sum[i % 4] = terms
            sum_tx[i] = terms.astype(jnp.bfloat16)
            for k in range(1, n_dp):
                sum_copy(i, k).start()

        @pl.when((i >= 1) & (i <= 8))
        def _():
            t = i - 1
            mine = pl.ds(pl.multiple_of(d * piece, piece), piece)
            total = own_sum[t % 4, mine, :]
            for k in range(1, n_dp):
                sum_copy(t, k).wait_recv()
                total = total + sum_rx[t, k - 1].astype(jnp.float32)
            hid[t, mine, :] = (total / (1.0 + jnp.exp(-total))).astype(jnp.bfloat16)
            for k in range(1, n_dp):
                hid_copy(t, k).start()

        @pl.when(is_mid & (i <= 6))
        def _():
            zz = source(i + 1)
            forward(i + 1, zz, xl).wait_recv()
            forward(i + 1, zz, xl).start()

        @pl.when((i >= 2) & (i <= 9))
        def _():
            t = i - 2
            zz = source(t)
            for k in range(1, n_dp):
                hid_copy(t, k).wait_recv()
            term[zz] = lax.dot_general(
                hid[t], down_v[...], (((0,), (0,)), ((), ())), preferred_element_type=jnp.float32
            )

            @pl.when(is_end & (t >= 1))
            def _():
                ret_tx[zz] = term[zz].astype(jnp.bfloat16)

            for x in range(2):
                @pl.when(is_end & ((t == 2) | (t == 5)))
                def _():
                    home_copy(zz, x, 0).start()

                @pl.when(is_end & (t == 1))
                def _():
                    root_copy(zz, x, 0, far).start()

                @pl.when(is_end & ((t == 3) | (t == 4) | (t >= 6)))
                def _():
                    joint_copy(zz, x, far).start()

        @pl.when(is_mid & (i <= 6))
        def _():
            zz = source(i + 1)
            forward(i + 1, zz, other).wait_recv()
            forward(i + 1, zz, other).start()

        def join(zz, x):
            block = slice(x * cap, (x + 1) * cap)
            joint_copy(zz, x, far).wait_recv()
            ret_tx[zz, block] = (term[zz, block] + joint[zz, block].astype(jnp.float32)).astype(jnp.bfloat16)

        @pl.when(is_mid & (i >= 6) & (i <= 10) & (i != 8))
        def _():
            u = i - 6
            zz = (z + nd * (u // 3 - u - 1) + Z) % Z
            for x in range(2):
                join(zz, x)

                @pl.when(i == 6)
                def _():
                    root_copy(zz, x, 1, far).start()

                @pl.when(i >= 7)
                def _():
                    joint_copy(zz, x, far).start()

        @pl.when(is_mid & ((i == 8) | (i >= 10)))
        def _():
            v = i - 8
            zz = (z + nd * (1 + v - v // 2) + Z) % Z
            for x in range(2):
                join(zz, x)

                @pl.when(i == 8)
                def _():
                    root_copy(zz, x, 1, near).start()

                @pl.when(i >= 10)
                def _():
                    home_copy(zz, x, 1).start()

        @pl.when(i == 9 - mid)
        def _():
            for x in (other, xl):
                block = pl.ds(pl.multiple_of(x * cap, cap), cap)
                root_copy(z, x, 1, far).wait_recv()
                total = term[z, block, :] + own_rx[1, block, :].astype(jnp.float32)

                @pl.when(is_end)
                def _():
                    ret_tx[z, block, :] = total.astype(jnp.bfloat16)

                @pl.when(is_mid)
                def _():
                    root_copy(z, x, 0, near).wait_recv()
                    ret_tx[z, block, :] = (total + own_rx[0, block, :].astype(jnp.float32)).astype(jnp.bfloat16)

                if x is other:
                    home_copy(z, other, 0).start()

        return carry

    lax.fori_loop(0, 12, each_step, 0)

    summed[pl.ds(pl.multiple_of(own_expert * cap, cap), cap), :] = ret_tx[z, pl.ds(pl.multiple_of(xl * cap, cap), cap), :]

    def arrival(e, place):
        return send(fin.at[e, place], fin.at[e, place], ret_send.at[0, 0], fin_recv.at[e, place], at(other, z))

    for x in (xl, other):
        e = 2 * x + 1 - g
        for place in range(2):
            arrival(e, place).wait_recv()
        summed[pl.ds(pl.multiple_of(e * cap, cap), cap), :] = (
            fin[e, 0].astype(jnp.float32) + fin[e, 1].astype(jnp.float32)
        ).astype(jnp.bfloat16)
    e = 2 * other + g
    arrival(e, 0).wait_recv()
    summed[pl.ds(pl.multiple_of(e * cap, cap), cap), :] = fin[e, 0]

    gate_value = 1.0 / (1.0 + jnp.exp(-jnp.sum(chosen[...] * stat_rx[...], axis=1, keepdims=True)))
    expert_out = jnp.dot(
        unplacer[...], summed[...], preferred_element_type=jnp.float32
    )
    out[...] = (arrived[...].astype(jnp.float32) + gate_value * expert_out).astype(jnp.bfloat16)

    raw_copy.wait_send()
    stat_copy.wait_send()
    for copy in (cross, ext_own, ext_other, own_sends[0], relay_sends[0]):
        copy.wait_send()

    @pl.when(is_mid)
    def _():
        own_sends[1].wait_send()
        relay_sends[1].wait_send()

    def sent(t, carry):
        zz = source(t)

        @pl.when(end_forwards(t) | ((t >= 1) & is_mid))
        def _():
            for x in range(2):
                forward(t, zz, x).wait_send()

        for k in range(1, n_dp):
            sum_copy(t, k).wait_send()
            hid_copy(t, k).wait_send()

        @pl.when(t >= 1)
        def _():
            for x in range(2):
                joint_copy(zz, x, far).wait_send()

        return carry

    lax.fori_loop(0, STEPS, sent, 0)
    home_copy(z, other, 0).wait_send()


def local(tokens, modality, routes, norm_gain, router, gate_weight, down_weight):
    tok, width = tokens.shape[1:]
    n_pipe, n_dp = lax.axis_size("pipe"), lax.axis_size("dp")
    part = width // n_dp
    cap = 2 * tok // router.shape[2]
    hidden = gate_weight.shape[2]
    piece = hidden // n_dp
    bf16, f32 = jnp.bfloat16, jnp.float32
    vmem = pl.BlockSpec(memory_space=pltpu.VMEM)
    anywhere = pl.BlockSpec(memory_space=pl.ANY)
    dma = pltpu.SemaphoreType.DMA
    result = pl.pallas_call(
        functools.partial(kernel, n_pipe, n_dp),
        out_shape=jax.ShapeDtypeStruct((tok, part), bf16),
        in_specs=[anywhere] * 7,
        out_specs=vmem,
        scratch_shapes=[
            pltpu.VMEM((1, tok), jnp.int32),
            pltpu.VMEM((1, tok), jnp.int32),
            pltpu.VMEM((1, width), f32),
            pltpu.VMEM((router.shape[0], router.shape[2], width), bf16),
            pltpu.VMEM((tok, width), bf16),
            pltpu.VMEM((tok, width), bf16),
            pltpu.VMEM((hidden, part), bf16),
            pltpu.VMEM((hidden, part), bf16),
            pltpu.VMEM((tok, part), bf16),
            pltpu.VMEM((tok, 128), f32),
            pltpu.VMEM((tok, 128), f32),
            pltpu.VMEM((4 * cap, tok), bf16),
            pltpu.VMEM((tok, 4 * cap), bf16),
            pltpu.VMEM((tok, 128), f32),
            pltpu.VMEM((3, cap, part), bf16),
            pltpu.VMEM((STEPS, 2 * cap, part), bf16),
            pltpu.VMEM((STEPS, hidden, 2 * cap), bf16),
            pltpu.VMEM((STEPS, n_dp - 1, piece, 2 * cap), bf16),
            pltpu.VMEM((4, hidden, 2 * cap), f32),
            pltpu.VMEM((STEPS, hidden, 2 * cap), bf16),
            pltpu.VMEM((STEPS, 2 * cap, part), f32),
            pltpu.VMEM((STEPS, 2 * cap, part), bf16),
            pltpu.VMEM((STEPS, 2 * cap, part), bf16),
            pltpu.VMEM((2, 2 * cap, part), bf16),
            pltpu.VMEM((4, 2, cap, part), bf16),
            pltpu.VMEM((4 * cap, part), bf16),
            dma((7,)),
            dma((2,)),
            dma((2,)),
            dma((7,)),
            dma((STEPS, 2)),
            dma((STEPS, 2)),
            dma((STEPS, n_dp - 1)),
            dma((STEPS, n_dp - 1)),
            dma((STEPS, n_dp - 1)),
            dma((STEPS, n_dp - 1)),
            dma((STEPS, 2)),
            dma((STEPS, 2)),
            dma((2, 2)),
            dma((4, 2)),
        ],
        compiler_params=pltpu.CompilerParams(
            collective_id=0, has_side_effects=True, vmem_limit_bytes=60 * 1024 * 1024
        ),
    )(
        tokens[0],
        modality,
        routes.reshape(1, tok),
        norm_gain.reshape(1, width),
        jnp.transpose(router, (0, 2, 1)),
        jnp.transpose(gate_weight[0]),
        down_weight[0],
    )
    return result[None]


def solution(mesh):
    placed = (
        P("pipe", "expert", None),
        P("pipe", "expert"),
        P("pipe", "expert", None),
        P(),
        P(),
        P("pipe", "dp", "expert"),
        P("pipe", "expert", "dp"),
    )
    return jax.shard_map(
        local, mesh=mesh, in_specs=placed, out_specs=P("pipe", "expert", "dp"), check_vma=False
    )
```

```python
import functools

import jax
import jax.numpy as jnp
from jax import lax
from jax.experimental import pallas as pl
from jax.experimental.pallas import tpu as pltpu
from jax.sharding import PartitionSpec as P

MESH = pl.DeviceIdType.MESH
epsilon = 1e-06
Z = 8
STEPS = 8


def kernel(
    n_pipe, n_dp,
    tokens, modality_hbm, routes_hbm, gain_hbm, router_hbm, gate_hbm, down_hbm,
    out,
    modality, routes, gain, router, tok_v, normed_v, gate_v, down_v, arrived, stat_tx, stat_rx, placer, unplacer, chosen,
    packed, recv, sum_tx, sum_rx, own_sum, hid, term, ret_tx, joint, own_rx, fin, summed,
    local_sem, pipe_send, pipe_recv, first_send, forward_send, dispatch_recv,
    sum_send, sum_recv, hid_send, hid_recv, ret_send, joint_recv, own_recv, fin_recv,
):
    tok = tok_v.shape[0]
    cap = recv.shape[1] // 2
    part = recv.shape[2]
    piece = sum_rx.shape[2]
    s, j, d = lax.axis_index("pipe"), lax.axis_index("expert"), lax.axis_index("dp")
    xl, z = j // Z, j % Z
    g, p = z // 4, z % 4
    mid = ((p + 1) // 2) % 2
    nd = 2 * (p // 2) - 1
    near, far = (z + nd + Z) % Z, (z - nd + Z) % Z
    entry = (z + nd * (1 + mid) + Z) % Z
    other = 1 - xl
    is_mid = mid == 1
    is_end = mid == 0

    def at(x, zz):
        return (s, x * Z + zz, d)

    def send(src, dst, send_sem, recv_sem, device):
        return pltpu.make_async_remote_copy(
            src_ref=src, dst_ref=dst, send_sem=send_sem, recv_sem=recv_sem,
            device_id=device, device_id_type=MESH,
        )

    def rows(ref, zz, x):
        return ref.at[zz, pl.ds(pl.multiple_of(x * cap, cap), cap)]

    tok_copy = pltpu.make_async_copy(tokens, tok_v, local_sem.at[0])
    gate_copy = pltpu.make_async_copy(gate_hbm, gate_v, local_sem.at[1])
    down_copy = pltpu.make_async_copy(down_hbm, down_v, local_sem.at[2])
    small = [
        pltpu.make_async_copy(a, b, local_sem.at[3 + k])
        for k, (a, b) in enumerate(((modality_hbm, modality), (routes_hbm, routes), (gain_hbm, gain), (router_hbm, router)))
    ]
    for copy in small:
        copy.start()
    tok_copy.start()

    barrier = pltpu.get_barrier_semaphore()
    partners = [
        ((s + 1) % n_pipe, j, d),
        ((s + n_pipe - 1) % n_pipe, j, d),
        at(other, z), at(xl, far),
    ] + [(s, j, (d + k) % n_dp) for k in range(1, n_dp)]
    for steps in (1 + 2 * mid, 2):
        partners += [at(x, (z + nd * steps + Z) % Z) for x in (xl, other)]
    for device in partners:
        pl.semaphore_signal(barrier, inc=1, device_id=device, device_id_type=MESH)

    @pl.when(is_mid)
    def _():
        pl.semaphore_signal(barrier, inc=1, device_id=at(xl, near), device_id_type=MESH)

    gate_copy.start()
    down_copy.start()
    for copy in small:
        copy.wait()

    route_row = routes[...]
    hits = (lax.broadcasted_iota(jnp.int32, (8, tok), 0) == route_row).astype(jnp.float32)
    before = (
        lax.broadcasted_iota(jnp.int32, (tok, tok), 0) < lax.broadcasted_iota(jnp.int32, (tok, tok), 1)
    ).astype(jnp.bfloat16)
    earlier = jnp.dot(hits.astype(jnp.bfloat16), before, preferred_element_type=jnp.float32)
    rank = jnp.sum(hits * earlier, axis=0, keepdims=True)
    slot_row = route_row.astype(jnp.float32) * cap + rank
    slots = lax.broadcasted_iota(jnp.int32, (4 * cap, tok), 0).astype(jnp.float32)
    placer[...] = (slots == slot_row).astype(jnp.bfloat16)
    slot_col = jnp.transpose(jnp.broadcast_to(slot_row, (tok, tok)))[:, 0:1]
    slots = lax.broadcasted_iota(jnp.int32, (tok, 4 * cap), 1).astype(jnp.float32)
    unplacer[...] = (slots == slot_col).astype(jnp.bfloat16)
    pick_row = (modality[...] * 4 + route_row).astype(jnp.float32)
    pick_col = jnp.transpose(jnp.broadcast_to(pick_row, (tok, tok)))[:, 0:1]
    lanes = lax.broadcasted_iota(jnp.int32, (tok, 128), 1).astype(jnp.float32)
    chosen[...] = (lanes == pick_col).astype(jnp.float32)

    pl.semaphore_wait(barrier, len(partners) + mid)

    following = ((s + 1) % n_pipe, j, d)
    own_columns = pl.ds(pl.multiple_of(d * part, part), part)
    raw_copy = send(tokens.at[:, own_columns], arrived, pipe_send.at[0], pipe_recv.at[0], following)
    raw_copy.start()

    stat_tx[...] = jnp.zeros_like(stat_tx)
    tok_copy.wait()

    def norm_rows(i, carry):
        block = pl.ds(pl.multiple_of(i * 16, 16), 16)
        x = tok_v[block, :].astype(jnp.float32)
        scale = lax.rsqrt(jnp.mean(x * x, axis=-1, keepdims=True) + epsilon)
        normed_v[block, :] = (x * scale * gain[...]).astype(jnp.bfloat16)
        stat_tx[block, 8:9] = scale
        return carry

    lax.fori_loop(0, tok // 16, norm_rows, 0)
    for kind in range(2):
        stat_tx[:, 4 * kind : 4 * kind + 4] = lax.dot_general(
            normed_v[...], router[kind], (((1,), (1,)), ((), ())), preferred_element_type=jnp.float32
        )
    stat_copy = send(stat_tx, stat_rx, pipe_send.at[1], pipe_recv.at[1], following)
    stat_copy.start()
    raw_copy.wait_recv()
    stat_copy.wait_recv()

    scale = stat_rx[:, 8:9]
    normed = (arrived[...].astype(jnp.float32) * scale * gain[:, own_columns]).astype(jnp.bfloat16)

    def pack(x, group):
        spot = pl.ds(pl.multiple_of((2 * x + group) * cap, cap), cap)
        return jnp.dot(placer[spot, :], normed, preferred_element_type=jnp.float32).astype(jnp.bfloat16)

    packed[0] = pack(other, g)
    cross = send(packed.at[0], rows(recv, z, xl), first_send.at[0], dispatch_recv.at[z, xl], at(other, z))
    cross.start()
    packed[1] = pack(xl, 1 - g)
    ext_own = send(packed.at[1], rows(recv, z, xl), first_send.at[1], dispatch_recv.at[z, xl], at(xl, entry))
    ext_own.start()
    packed[2] = pack(other, 1 - g)
    ext_other = send(packed.at[2], rows(recv, z, xl), first_send.at[2], dispatch_recv.at[z, xl], at(other, entry))
    ext_other.start()
    recv[z, pl.ds(pl.multiple_of(xl * cap, cap), cap), :] = pack(xl, g)

    def inside(x, first):
        block = rows(recv, z, x)
        return [
            send(block, block, first_send.at[first + k], dispatch_recv.at[z, x], at(xl, target))
            for k, target in enumerate((far, near))
        ]

    own_sends, relay_sends = inside(xl, 3), inside(other, 5)

    def start_inside(copies):
        copies[0].start()

        @pl.when(is_mid)
        def _():
            copies[1].start()

    start_inside(own_sends)
    relay_sends[0].wait_recv()
    start_inside(relay_sends)

    gate_copy.wait()
    down_copy.wait()

    def source(t):
        at_mid = (t % 2) * ((t + 1) // 2) - (1 - t % 2) * (t // 2)
        at_end = sum(
            offset * (1 - ((t - k) * (t - k) + 48) // 49) for k, offset in enumerate((0, -1, 1, -2, -3, 2, -4, -5))
        )
        return (z + nd * (mid * at_mid + (1 - mid) * at_end) + 2 * Z) % Z

    def passed_on(t):
        return (z + nd * ((t + 1) // 2) + Z) % Z

    def forward(t, zz, x):
        to_near = mid * (1 - (t % 2) * (1 - t // 7))
        target = (z + nd * (2 * to_near - 1) + Z) % Z
        return send(rows(recv, zz, x), rows(recv, zz, x), forward_send.at[t, x], dispatch_recv.at[zz, x], at(xl, target))

    def end_forwards(t):
        return is_end & ((t == 1) | (t == 3))

    def span(ref, t, q):
        return ref.at[t, pl.ds(pl.multiple_of(q * piece, piece), piece)]

    def sum_copy(t, k):
        q = (d + k) % n_dp
        return send(span(sum_tx, t, q), sum_rx.at[t, k - 1], sum_send.at[t, k - 1], sum_recv.at[t, k - 1], (s, j, q))

    def hid_copy(t, k):
        own = span(hid, t, d)
        return send(own, own, hid_send.at[t, k - 1], hid_recv.at[t, k - 1], (s, j, (d + k) % n_dp))

    own_expert = 2 * xl + g

    def joint_copy(zz, x, target):
        return send(rows(ret_tx, zz, x), rows(joint, zz, x), ret_send.at[zz, x], joint_recv.at[zz, x], at(xl, target))

    def root_copy(zz, x, place, target):
        return send(rows(ret_tx, zz, x), rows(own_rx, place, x), ret_send.at[zz, x], own_recv.at[place, x], at(xl, target))

    def home_copy(zz, x, place):
        return send(rows(ret_tx, zz, x), fin.at[own_expert, place], ret_send.at[zz, x], fin_recv.at[own_expert, place], at(x, zz))

    def each_step(i, carry):
        @pl.when(i <= 7)
        def _():
            @pl.when(end_forwards(i))
            def _():
                for x in (xl, other):
                    forward(i, passed_on(i), x).wait_recv()
                    forward(i, passed_on(i), x).start()

            zz = source(i)
            for x in (xl, other):
                @pl.when(is_end & (i >= 1) & (i != 2) & (i != 5))
                def _():
                    forward(i, zz, x).wait_recv()

            terms = lax.dot_general(
                gate_v[...], recv[zz], (((1,), (1,)), ((), ())), preferred_element_type=jnp.float32
            )
            own_sum[i % 4] = terms
            sum_tx[i] = terms.astype(jnp.bfloat16)
            for k in range(1, n_dp):
                sum_copy(i, k).start()

        @pl.when((i >= 1) & (i <= 8))
        def _():
            t = i - 1
            mine = pl.ds(pl.multiple_of(d * piece, piece), piece)
            total = own_sum[t % 4, mine, :]
            for k in range(1, n_dp):
                sum_copy(t, k).wait_recv()
                total = total + sum_rx[t, k - 1].astype(jnp.float32)
            hid[t, mine, :] = (total / (1.0 + jnp.exp(-total))).astype(jnp.bfloat16)
            for k in range(1, n_dp):
                hid_copy(t, k).start()

        @pl.when(is_mid & (i <= 6))
        def _():
            zz = source(i + 1)
            forward(i + 1, zz, xl).wait_recv()
            forward(i + 1, zz, xl).start()

        @pl.when((i >= 2) & (i <= 9))
        def _():
            t = i - 2
            zz = source(t)
            for k in range(1, n_dp):
                hid_copy(t, k).wait_recv()
            term[zz] = lax.dot_general(
                hid[t], down_v[...], (((0,), (0,)), ((), ())), preferred_element_type=jnp.float32
            )

            @pl.when(is_end & (t >= 1))
            def _():
                ret_tx[zz] = term[zz].astype(jnp.bfloat16)

            for x in range(2):
                @pl.when(is_end & ((t == 2) | (t == 5)))
                def _():
                    home_copy(zz, x, 0).start()

                @pl.when(is_end & (t == 1))
                def _():
                    root_copy(zz, x, 0, far).start()

                @pl.when(is_end & ((t == 3) | (t == 4) | (t >= 6)))
                def _():
                    joint_copy(zz, x, far).start()

        @pl.when(is_mid & (i <= 6))
        def _():
            zz = source(i + 1)
            forward(i + 1, zz, other).wait_recv()
            forward(i + 1, zz, other).start()

        def join(zz, x):
            block = slice(x * cap, (x + 1) * cap)
            joint_copy(zz, x, far).wait_recv()
            ret_tx[zz, block] = (term[zz, block] + joint[zz, block].astype(jnp.float32)).astype(jnp.bfloat16)

        @pl.when(is_mid & (i >= 6) & (i <= 10) & (i != 8))
        def _():
            u = i - 6
            zz = (z + nd * (u // 3 - u - 1) + Z) % Z
            for x in range(2):
                join(zz, x)

                @pl.when(i == 6)
                def _():
                    root_copy(zz, x, 1, far).start()

                @pl.when(i >= 7)
                def _():
                    joint_copy(zz, x, far).start()

        @pl.when(is_mid & ((i == 8) | (i >= 10)))
        def _():
            v = i - 8
            zz = (z + nd * (1 + v - v // 2) + Z) % Z
            for x in range(2):
                join(zz, x)

                @pl.when(i == 8)
                def _():
                    root_copy(zz, x, 1, near).start()

                @pl.when(i >= 10)
                def _():
                    home_copy(zz, x, 1).start()

        @pl.when(i == 9 - mid)
        def _():
            for x in (other, xl):
                block = pl.ds(pl.multiple_of(x * cap, cap), cap)
                root_copy(z, x, 1, far).wait_recv()
                total = term[z, block, :] + own_rx[1, block, :].astype(jnp.float32)

                @pl.when(is_end)
                def _():
                    ret_tx[z, block, :] = total.astype(jnp.bfloat16)

                @pl.when(is_mid)
                def _():
                    root_copy(z, x, 0, near).wait_recv()
                    ret_tx[z, block, :] = (total + own_rx[0, block, :].astype(jnp.float32)).astype(jnp.bfloat16)

                if x is other:
                    home_copy(z, other, 0).start()

        return carry

    lax.fori_loop(0, 12, each_step, 0)

    raw_copy.wait_send()
    stat_copy.wait_send()
    for copy in (cross, ext_own, ext_other, own_sends[0], relay_sends[0]):
        copy.wait_send()

    @pl.when(is_mid)
    def _():
        own_sends[1].wait_send()
        relay_sends[1].wait_send()

    def sent(t, carry):
        zz = source(t)

        @pl.when(end_forwards(t) | ((t >= 1) & is_mid))
        def _():
            for x in range(2):
                forward(t, zz, x).wait_send()

        for k in range(1, n_dp):
            sum_copy(t, k).wait_send()
            hid_copy(t, k).wait_send()

        return carry

    lax.fori_loop(0, STEPS, sent, 0)

    gate_value = 1.0 / (1.0 + jnp.exp(-jnp.sum(chosen[...] * stat_rx[...], axis=1, keepdims=True)))
    summed[pl.ds(pl.multiple_of(own_expert * cap, cap), cap), :] = ret_tx[z, pl.ds(pl.multiple_of(xl * cap, cap), cap), :]

    def arrival(e, place):
        return send(fin.at[e, place], fin.at[e, place], ret_send.at[0, 0], fin_recv.at[e, place], at(other, z))

    for x in (xl, other):
        e = 2 * x + 1 - g
        for place in range(2):
            arrival(e, place).wait_recv()
        summed[pl.ds(pl.multiple_of(e * cap, cap), cap), :] = (
            fin[e, 0].astype(jnp.float32) + fin[e, 1].astype(jnp.float32)
        ).astype(jnp.bfloat16)
    e = 2 * other + g
    arrival(e, 0).wait_recv()
    summed[pl.ds(pl.multiple_of(e * cap, cap), cap), :] = fin[e, 0]

    expert_out = jnp.dot(
        unplacer[...], summed[...], preferred_element_type=jnp.float32
    )
    out[...] = (arrived[...].astype(jnp.float32) + gate_value * expert_out).astype(jnp.bfloat16)

    def returned(t, carry):
        for x in range(2):
            joint_copy(source(t), x, far).wait_send()
        return carry

    lax.fori_loop(1, STEPS, returned, 0)
    home_copy(z, other, 0).wait_send()


def local(tokens, modality, routes, norm_gain, router, gate_weight, down_weight):
    tok, width = tokens.shape[1:]
    n_pipe, n_dp = lax.axis_size("pipe"), lax.axis_size("dp")
    part = width // n_dp
    cap = 2 * tok // router.shape[2]
    hidden = gate_weight.shape[2]
    piece = hidden // n_dp
    bf16, f32 = jnp.bfloat16, jnp.float32
    vmem = pl.BlockSpec(memory_space=pltpu.VMEM)
    anywhere = pl.BlockSpec(memory_space=pl.ANY)
    dma = pltpu.SemaphoreType.DMA
    result = pl.pallas_call(
        functools.partial(kernel, n_pipe, n_dp),
        out_shape=jax.ShapeDtypeStruct((tok, part), bf16),
        in_specs=[anywhere] * 7,
        out_specs=vmem,
        scratch_shapes=[
            pltpu.VMEM((1, tok), jnp.int32),
            pltpu.VMEM((1, tok), jnp.int32),
            pltpu.VMEM((1, width), f32),
            pltpu.VMEM((router.shape[0], router.shape[2], width), bf16),
            pltpu.VMEM((tok, width), bf16),
            pltpu.VMEM((tok, width), bf16),
            pltpu.VMEM((hidden, part), bf16),
            pltpu.VMEM((hidden, part), bf16),
            pltpu.VMEM((tok, part), bf16),
            pltpu.VMEM((tok, 128), f32),
            pltpu.VMEM((tok, 128), f32),
            pltpu.VMEM((4 * cap, tok), bf16),
            pltpu.VMEM((tok, 4 * cap), bf16),
            pltpu.VMEM((tok, 128), f32),
            pltpu.VMEM((3, cap, part), bf16),
            pltpu.VMEM((STEPS, 2 * cap, part), bf16),
            pltpu.VMEM((STEPS, hidden, 2 * cap), bf16),
            pltpu.VMEM((STEPS, n_dp - 1, piece, 2 * cap), bf16),
            pltpu.VMEM((4, hidden, 2 * cap), f32),
            pltpu.VMEM((STEPS, hidden, 2 * cap), bf16),
            pltpu.VMEM((STEPS, 2 * cap, part), f32),
            pltpu.VMEM((STEPS, 2 * cap, part), bf16),
            pltpu.VMEM((STEPS, 2 * cap, part), bf16),
            pltpu.VMEM((2, 2 * cap, part), bf16),
            pltpu.VMEM((4, 2, cap, part), bf16),
            pltpu.VMEM((4 * cap, part), bf16),
            dma((7,)),
            dma((2,)),
            dma((2,)),
            dma((7,)),
            dma((STEPS, 2)),
            dma((STEPS, 2)),
            dma((STEPS, n_dp - 1)),
            dma((STEPS, n_dp - 1)),
            dma((STEPS, n_dp - 1)),
            dma((STEPS, n_dp - 1)),
            dma((STEPS, 2)),
            dma((STEPS, 2)),
            dma((2, 2)),
            dma((4, 2)),
        ],
        compiler_params=pltpu.CompilerParams(
            collective_id=0, has_side_effects=True, vmem_limit_bytes=60 * 1024 * 1024
        ),
    )(
        tokens[0],
        modality,
        routes.reshape(1, tok),
        norm_gain.reshape(1, width),
        jnp.transpose(router, (0, 2, 1)),
        jnp.transpose(gate_weight[0]),
        down_weight[0],
    )
    return result[None]


def solution(mesh):
    placed = (
        P("pipe", "expert", None),
        P("pipe", "expert"),
        P("pipe", "expert", None),
        P(),
        P(),
        P("pipe", "dp", "expert"),
        P("pipe", "expert", "dp"),
    )
    return jax.shard_map(
        local, mesh=mesh, in_specs=placed, out_specs=P("pipe", "expert", "dp"), check_vma=False
    )
```
